256 devices in a mesh: dp: 32 (over y, x, core), feat: 8 (over z).
Axes of the slice: x: 4, y: 4, z: 8, core: 2. Of those that a mesh axis runs over, the one named last changes fastest.
Arguments:
- view_a: bfloat16 [8192, 4096], P('dp', 'feat'), may hold values from -51 to 51, as said below
- view_b: bfloat16 [8192, 4096], P('dp', 'feat'), may hold values from -51 to 51, as said below
Outputs:
- grad_a: bfloat16 [8192, 4096], P('dp', 'feat')
- grad_b: bfloat16 [8192, 4096], P('dp', 'feat')
- loss_value: float32 [], replicated
The draws below stay inside these ranges and needn't reach their ends.
Inputs may be any that keep to these rules, and one draw needn't show every extreme that they name: `view_a`: Real-valued projector outputs. `view_b`: Real-valued projector outputs.
All inputs are finite; a program needn't handle non-finite values.
Results may differ from the reference program's by a relative error of at most 0.0083.
Values may be sent and summed in bfloat16 or wider, within the bound.
No kernel may reach another device: no remote copies, remote signals or barrier semaphores. Data moves between devices by JAX's collectives and lax.ppermute only.
A program may use at most 64 MiB of HBM per device.

```python
import math
import jax
import jax.numpy as jnp
from jax import lax

D = 4096
BATCH = 8192


def shared_field(key, offset_spread):
    subkeys = jax.random.split(key, 6)
    latent = jax.random.truncated_normal(subkeys[0], -4.0, 4.0, (BATCH, D), jnp.float32)
    offset_by = jax.random.randint(subkeys[1], (), D // 4, 3 * D // 4)
    mixing = jax.random.uniform(subkeys[2], (D,), jnp.float32, 0.3, 0.9)
    common = latent + mixing * jnp.roll(latent, offset_by, axis=1)
    scales = jnp.exp(jax.random.uniform(subkeys[3], (D,), jnp.float32, math.log(0.5), math.log(4.0)))
    offsets = offset_spread * jax.random.truncated_normal(subkeys[4], -4.0, 4.0, (D,), jnp.float32)
    levels = jnp.exp(jax.random.uniform(subkeys[5], (D,), jnp.float32, math.log(0.05), math.log(0.5)))
    return (common, scales, offsets, levels)


def draw_view_a(key, part):
    shared = shared_field(key, 0.5)
    key = jax.random.fold_in(key, 11)
    common, scales, offsets, levels = shared
    own_noise = jax.random.truncated_normal(key, -4.0, 4.0, (BATCH, D), jnp.float32)
    return ((common + levels * own_noise) * scales + offsets).astype(jnp.bfloat16)


def draw_view_b(key, part):
    shared = shared_field(key, 0.5)
    key = jax.random.fold_in(key, 23)
    common, scales, offsets, levels = shared
    own_noise = jax.random.truncated_normal(key, -4.0, 4.0, (BATCH, D), jnp.float32)
    return ((common + levels * own_noise) * scales + offsets).astype(jnp.bfloat16)


def setup_inputs(seed: int = 0) -> dict:
    splits = jax.random.split(jax.random.key(seed), 3)
    return {
        "view_a": draw_view_a(jax.random.fold_in(splits[2], 71), 0),
        "view_b": draw_view_b(jax.random.fold_in(splits[2], 71), 0),
    }


OFF_WEIGHT = 0.0051
EPSILON = 1e-05

def whiten(view_data, images):
    values = view_data.astype(jnp.float32)
    centre = lax.optimization_barrier(jnp.sum(values, axis=0)) / images
    shifted = values - centre
    spread_inv = lax.rsqrt(lax.optimization_barrier(jnp.sum(shifted * shifted, axis=0)) / images + EPSILON)
    return (shifted * spread_inv, spread_inv)

def finish_grad(back, white, spread_inv, images):
    centre = lax.optimization_barrier(jnp.sum(back, axis=0)) / images
    along = lax.optimization_barrier(jnp.sum(back * white, axis=0)) / images
    return (spread_inv * (back - centre - white * along)).astype(jnp.bfloat16)

def reference(view_a, view_b):
    images = view_a.shape[0]
    white_a, inv_a = whiten(view_a, images)
    white_b, inv_b = whiten(view_b, images)
    norm_a = white_a.astype(jnp.bfloat16)
    norm_b = white_b.astype(jnp.bfloat16)
    correlation = lax.dot_general(norm_a, norm_b, (((0,), (0,)), ((), ())), preferred_element_type=jnp.float32) / images
    row_ids = jnp.arange(D, dtype=jnp.int32)[:, None]
    col_ids = jnp.arange(D, dtype=jnp.int32)[None, :]
    on_diagonal = row_ids == col_ids
    deficit = 1.0 - correlation
    loss_value = jnp.sum(jnp.where(on_diagonal, deficit * deficit, OFF_WEIGHT * correlation * correlation))
    pull_grad = jnp.where(on_diagonal, -2.0 * deficit, 2.0 * OFF_WEIGHT * correlation).astype(jnp.bfloat16)
    back_a = lax.dot_general(norm_b, pull_grad, (((1,), (1,)), ((), ())), preferred_element_type=jnp.float32)
    back_b = jnp.dot(norm_a, pull_grad, preferred_element_type=jnp.float32)
    grad_a = finish_grad(back_a, white_a, inv_a, images)
    grad_b = finish_grad(back_b, white_b, inv_b, images)
    return (grad_a, grad_b, loss_value)
```

```python
import jax
import jax.numpy as jnp
from jax import lax
from jax.sharding import Mesh, PartitionSpec as P

OFF_WEIGHT = 0.0051
EPSILON = 1e-05
F32 = jnp.float32
BF16 = jnp.bfloat16
PLANE = ("y", "x")


def turn(size, step):
    return [(i, (i + step) % size) for i in range(size)]


def shift(value, axis, step):
    return lax.ppermute(value, axis, turn(lax.axis_size(axis), step))


def swap(value):
    return lax.ppermute(value, "c", [(0, 1), (1, 0)])


def spread(value, axes, size):
    copies = jnp.broadcast_to(value[None], (size,) + value.shape)
    return lax.all_to_all(copies, axes, split_axis=0, concat_axis=0, tiled=True)


def rotate(value, by):
    twice = jnp.concatenate([value, value], axis=0)
    return lax.dynamic_slice_in_dim(twice, by % value.shape[0], value.shape[0], axis=0)


def others(value, axis):
    return [shift(value, axis, step) for step in (1, 3, 2)]


def local(view_a, view_b):
    rows, width = view_a.shape
    y_size, x_size = lax.axis_size("y"), lax.axis_size("x")
    z_size = lax.axis_size("z")
    chips = y_size * x_size
    images = rows * 2 * chips
    width_all = width * z_size
    half = width // 2
    quarter = half // 4
    x_at, y_at, c_at, z_at = (lax.axis_index(name) for name in ("x", "y", "c", "z"))

    raw_b = lax.all_gather(view_b, "z", axis=1, tiled=True)
    late_a, _ = lax.optimization_barrier((view_a, raw_b))
    raw_a = lax.all_gather(late_a, "z", axis=1, tiled=True)

    values_a = view_a.astype(F32)
    values_b = view_b.astype(F32)
    local_a = jnp.sum(values_a, axis=0) / rows
    local_b = jnp.sum(values_b, axis=0) / rows
    apart_a = values_a - local_a
    apart_b = values_b - local_b
    mine = jnp.stack(
        [
            local_a,
            local_b,
            jnp.sum(apart_a * apart_a, axis=0),
            jnp.sum(apart_b * apart_b, axis=0),
            jnp.sum(apart_a * apart_b, axis=0),
        ]
    )
    pair = swap(mine)
    gap = mine[:2] - pair[:2]
    joined = jnp.concatenate(
        [
            (mine[:2] + pair[:2]) * 0.5,
            mine[2:4] + pair[2:4] + gap * gap * (rows / 2),
            mine[4:] + pair[4:] + gap[:1] * gap[1:] * (rows / 2),
        ]
    )
    all_stats = spread(joined, PLANE, chips)
    means = jnp.sum(all_stats[:, :2], axis=0) / chips
    away = all_stats[:, :2] - means
    squares = jnp.sum(all_stats[:, 2:4] + 2 * rows * away * away, axis=0)
    cross = jnp.sum(all_stats[:, 4] + 2 * rows * away[:, 0] * away[:, 1], axis=0)
    inverse = lax.rsqrt(squares / images + EPSILON)
    on_diagonal = cross / images * inverse[0] * inverse[1]
    pull_diagonal = -2.0 * (1.0 - on_diagonal)
    white_a = (values_a - means[0]) * inverse[0]
    white_b = (values_b - means[1]) * inverse[1]
    norm_a = white_a.astype(BF16)
    norm_b = white_b.astype(BF16)
    left = jnp.stack([jnp.sum(norm_a.astype(F32), axis=0), jnp.sum(norm_b.astype(F32), axis=0)])
    left = jnp.sum(spread(left + swap(left), PLANE, chips), axis=0)

    wide = spread(jnp.concatenate([means, inverse, left]), "z", z_size)
    wide = wide.transpose(1, 0, 2).reshape(6, width_all)
    wide_b = ((raw_b.astype(F32) - wide[1]) * wide[3]).astype(BF16)
    wide_a = ((raw_a.astype(F32) - wide[0]) * wide[2]).astype(BF16)

    keep = lax.dynamic_slice_in_dim(norm_a, c_at * half, half, axis=1)
    give = lax.dynamic_slice_in_dim(norm_a, (1 - c_at) * half, half, axis=1)
    chip_a = jnp.concatenate([keep, swap(give)], axis=0).T.reshape(4, quarter, 2 * rows)
    chip_b = jnp.concatenate([wide_b, swap(wide_b)], axis=0)
    chip_b = chip_b.reshape(2 * rows, z_size, 2, half)

    def tile(place, first, first_at, second):
        lhs = rotate(chip_a, first_at).reshape(half, 2 * rows)
        rhs = chip_b[:, :, place].reshape(2 * rows, z_size * half)
        part = jnp.dot(lhs, rhs, preferred_element_type=F32).astype(BF16)
        part = part.reshape(4, quarter, z_size * half)
        total = part[0].astype(F32)
        for step in (1, 3, 2):
            total = total + shift(part[step], first, step).astype(F32)
        total = total.astype(BF16)
        ahead, behind, across = others(total, second)
        total = (total.astype(F32) + across.astype(F32)) + (
            ahead.astype(F32) + behind.astype(F32)
        )
        row = lax.broadcasted_iota(jnp.int32, total.shape, 0)
        col = lax.broadcasted_iota(jnp.int32, total.shape, 1)
        own = (col == row + z_at * half + first_at * quarter) & (c_at == place)
        return jnp.where(own, 0.0, 2.0 * OFF_WEIGHT / images * total).astype(BF16)

    def collect(piece, axis, at):
        ahead, behind, across = others(piece, axis)
        pieces = jnp.stack([piece, behind, across, ahead])
        return rotate(pieces, (4 - at))

    pull_0 = tile(0, "x", x_at, "y")
    pull_1 = tile(1, "y", y_at, "x")

    outward = jnp.stack([pull_0, pull_1]).reshape(2, quarter, z_size, half)
    inward = lax.all_to_all(
        outward.transpose(2, 0, 1, 3), "z", split_axis=0, concat_axis=0, tiled=True
    )

    def both(value):
        other = swap(value)
        return jnp.where(
            c_at == 0, jnp.stack([value, other]), jnp.stack([other, value])
        )

    rows_0 = both(collect(pull_0, "x", x_at)).reshape(width, z_size, half)
    rows_1 = both(collect(pull_1, "y", y_at)).reshape(width, z_size, half)
    pull_rows = jnp.stack([rows_0, rows_1], axis=2).reshape(width, width_all)

    cols_0 = both(collect(inward[:, 0], "x", x_at))
    cols_1 = both(collect(inward[:, 1], "y", y_at))
    pull_cols = jnp.concatenate([cols_0, cols_1], axis=-1)
    pull_cols = pull_cols.transpose(2, 0, 1, 3, 4).reshape(width_all, width)

    back_a = lax.dot_general(
        wide_b, pull_rows, (((1,), (1,)), ((), ())), preferred_element_type=F32
    )
    back_b = jnp.dot(wide_a, pull_cols, preferred_element_type=F32)
    back_a = back_a + norm_b.astype(F32) * pull_diagonal
    back_b = back_b + norm_a.astype(F32) * pull_diagonal

    rows_f = pull_rows.astype(F32)
    cols_f = pull_cols.astype(F32)
    own = pull_diagonal * on_diagonal
    row_weight = jnp.sum(rows_f * rows_f, axis=1) / (2.0 * OFF_WEIGHT)
    col_weight = jnp.sum(cols_f * cols_f, axis=0) / (2.0 * OFF_WEIGHT)
    along_a = row_weight + own
    along_b = col_weight + own
    centre_a = (jnp.sum(rows_f * wide[5], axis=1) + pull_diagonal * left[1]) / images
    centre_b = (jnp.sum(cols_f * wide[4][:, None], axis=0) + pull_diagonal * left[0]) / images
    deficit = 1.0 - on_diagonal
    share = jnp.sum(0.5 * row_weight + deficit * deficit)
    loss_value = jnp.sum(spread(jnp.full((1, 128), share), "z", z_size)[:, 0, 0])
    grad_a = (inverse[0] * (back_a - centre_a - white_a * along_a)).astype(BF16)
    grad_b = (inverse[1] * (back_b - centre_b - white_b * along_b)).astype(BF16)
    return (grad_a, grad_b, loss_value)


def solution(mesh):
    split = P(("y", "x", "c"), "z")
    chips = Mesh(mesh.devices.reshape(4, 4, 2, 8), ("y", "x", "c", "z"))
    return jax.shard_map(
        local,
        mesh=chips,
        in_specs=(split, split),
        out_specs=(split, split, P()),
        check_vma=False,
    )
```

```python
import functools

import jax
import jax.numpy as jnp
from jax import lax
from jax.experimental import pallas as pl
from jax.experimental.pallas import tpu as pltpu
from jax.sharding import Mesh, PartitionSpec as P

OFF_WEIGHT = 0.0051
EPSILON = 1e-05
F32 = jnp.float32
BF16 = jnp.bfloat16
PLANE = ("y", "x")
CONTRACT_LAST = (((1,), (1,)), ((), ()))
EXTRA = 16
MIB = 1 << 20
VMEM = pl.BlockSpec(memory_space=pltpu.VMEM)
SMEM = pl.BlockSpec(memory_space=pltpu.SMEM)


def turn(size, step):
    return [(i, (i + step) % size) for i in range(size)]


def shift(value, axis, step):
    return lax.ppermute(value, axis, turn(lax.axis_size(axis), step))


def swap(value):
    return lax.ppermute(value, "c", [(0, 1), (1, 0)])


def spread(value, axes, size):
    copies = jnp.broadcast_to(value[None], (size,) + value.shape)
    return lax.all_to_all(copies, axes, split_axis=0, concat_axis=0, tiled=True)


def rotate(value, by):
    twice = jnp.concatenate([value, value], axis=0)
    return lax.dynamic_slice_in_dim(twice, by, value.shape[0], axis=0)


def others(value, axis):
    return [shift(value, axis, step) for step in (1, 3, 2)]


def normalise(raw, mean, inverse):
    return ((raw.astype(F32) - mean) * inverse).astype(BF16)


def correlate_body(stats, own, other, lhs_x, lhs_y, wide, *parts):
    mean, inverse = stats[0, 1:2], stats[0, 3:4]
    near = normalise(own[0], mean, inverse)
    wide[0] = near
    both = jnp.concatenate([near, normalise(other[0], mean, inverse)], axis=0)
    half = lhs_x.shape[0]
    quarter = half // 4
    for place, lhs in enumerate((lhs_x, lhs_y)):
        rhs = both[:, place * half : (place + 1) * half]
        part = jnp.dot(lhs[...], rhs, preferred_element_type=F32).astype(BF16)
        for turned in range(4):
            parts[4 * place + turned][...] = part[turned * quarter : (turned + 1) * quarter]


def correlate(stats, own, other, lhs_x, lhs_y):
    blocks, rows, width = own.shape
    half = width // 2
    quarter = half // 4
    block = pl.BlockSpec((1, rows, width), lambda g: (g, 0, 0))
    lhs = pl.BlockSpec((half, 2 * rows), lambda g: (0, 0))
    part = pl.BlockSpec((quarter, half), lambda g: (0, g))
    return pl.pallas_call(
        correlate_body,
        grid=(blocks,),
        in_specs=[
            pl.BlockSpec((1, 4, width), lambda g: (g, 0, 0)),
            block,
            block,
            lhs,
            lhs,
        ],
        out_specs=[block] + [part] * 8,
        out_shape=[jax.ShapeDtypeStruct(own.shape, BF16)]
        + [jax.ShapeDtypeStruct((quarter, blocks * half), BF16)] * 8,
        compiler_params=pltpu.CompilerParams(vmem_limit_bytes=16 * MIB),
        cost_estimate=pl.CostEstimate(
            flops=4 * rows * half * width * blocks, bytes_accessed=8 * MIB, transcendentals=0
        ),
        name="correlate",
    )(stats, own, other, lhs_x, lhs_y)


def tile_body(scale, at, *refs):
    inputs, (pull_0, pull_1, outward) = refs[:8], refs[8:]
    x_at, y_at, c_at, z_at = at[0], at[1], at[2], at[3]
    blocks, _, quarter, half = outward.shape
    for place, pull in enumerate((pull_0, pull_1)):
        own, ahead, behind, across = inputs[4 * place : 4 * place + 4]
        first_at = y_at if place else x_at
        row = lax.broadcasted_iota(jnp.int32, (quarter, half), 0)
        col = lax.broadcasted_iota(jnp.int32, (quarter, half), 1)
        same = (col == row + first_at * quarter) & (c_at == place)
        for g in range(blocks):
            cols = slice(g * half, (g + 1) * half)
            total = (own[:, cols].astype(F32) + across[:, cols].astype(F32)) + (
                ahead[:, cols].astype(F32) + behind[:, cols].astype(F32)
            )
            value = jnp.where(same & (z_at == g), 0.0, scale * total).astype(BF16)
            pull[:, cols] = value
            outward[g, place] = value


def make_tile(at, scale, first, second):
    quarter, wide = first[0].shape
    half = 4 * quarter
    piece = jax.ShapeDtypeStruct((quarter, wide), BF16)
    return pl.pallas_call(
        functools.partial(tile_body, scale),
        in_specs=[SMEM] + [VMEM] * 8,
        out_specs=[VMEM] * 3,
        out_shape=[
            piece,
            piece,
            jax.ShapeDtypeStruct((wide // half, 2, quarter, half), BF16),
        ],
        compiler_params=pltpu.CompilerParams(vmem_limit_bytes=16 * MIB),
        cost_estimate=pl.CostEstimate(
            flops=12 * quarter * wide, bytes_accessed=3 * MIB, transcendentals=0
        ),
        name="tile",
    )(at, *first, *second)


def pack_rows_body(at, *refs):
    pieces, out = refs[:8], refs[8]
    blocks, half, width = out.shape
    quarter = half // 4
    for place in range(2):
        for turned in range(4):
            spot = lax.rem(at[place] + turned, 4) * quarter
            rows = pl.ds(pl.multiple_of(spot, quarter), quarter)
            piece = pieces[4 * place + turned]
            for g in range(blocks):
                out[g, rows, place * half : (place + 1) * half] = piece[
                    :, g * half : (g + 1) * half
                ]


def pack_cols_body(at, inward, *refs):
    pieces, out = refs[:6], refs[6]
    blocks, half, width = out.shape
    quarter = half // 4
    for place in range(2):
        for turned in range(4):
            spot = lax.rem(at[place] + turned, 4) * quarter
            rows = pl.ds(pl.multiple_of(spot, quarter), quarter)
            for g in range(blocks):
                if turned:
                    value = pieces[3 * place + turned - 1][g]
                else:
                    value = inward[g, place]
                out[g, rows, place * half : (place + 1) * half] = value


def pack(body, at, shape, name, *pieces):
    return pl.pallas_call(
        body,
        in_specs=[SMEM] + [VMEM] * len(pieces),
        out_specs=VMEM,
        out_shape=jax.ShapeDtypeStruct(shape, BF16),
        compiler_params=pltpu.CompilerParams(vmem_limit_bytes=16 * MIB),
        cost_estimate=pl.CostEstimate(flops=0, bytes_accessed=4 * MIB, transcendentals=0),
        name=name,
    )(at, *pieces)


def finish(view, norm, vec, total, weight, mean_row, left_row, images):
    mean, inverse = vec[mean_row : mean_row + 1], vec[mean_row + 2 : mean_row + 3]
    pull, match, left = vec[4:5], vec[5:6], vec[left_row : left_row + 1]
    rows = view.shape[0]
    back = total[:rows] + norm.astype(F32) * pull
    centre = (total[rows : rows + 1] + pull * left) * (1.0 / images)
    along = weight + pull * match
    white = (view.astype(F32) - mean) * inverse
    return (inverse * (back - centre - white * along)).astype(BF16)


def rows_body(images, at, wide, sums, near, far, view, norm, vec, grad, weight, total):
    blocks, half, width = near.shape
    squares = jnp.ones((EXTRA, width), BF16)
    for which, pull in enumerate((near, far)):
        spot = (1 - at[2] if which else at[2]) * half
        cols = pl.ds(pl.multiple_of(spot, half), half)
        for g in range(blocks):
            extra = jnp.broadcast_to(sums[g, 1:2], (EXTRA, width)).astype(BF16)
            lhs = jnp.concatenate([wide[g], extra], axis=0)
            rhs = pull[g]
            wide_rhs = rhs.astype(F32)
            part = lax.dot_general(lhs, rhs, CONTRACT_LAST, preferred_element_type=F32)
            size = lax.dot_general(
                squares,
                (wide_rhs * wide_rhs).astype(BF16),
                CONTRACT_LAST,
                preferred_element_type=F32,
            )[:8]
            if g:
                total[:, cols] += part
                weight[:, cols] += size
            else:
                total[:, cols] = part
                weight[:, cols] = size
    weight[...] = weight[...] * (0.5 / OFF_WEIGHT)
    grad[...] = finish(
        view[...], norm[...], vec[...], total[...], weight[0:1], 0, 7, images
    )


def cols_body(images, at, wide, sums, near, far, view, norm, vec, grad, total):
    blocks, half, width = near.shape
    size = jnp.zeros((1, width), F32)
    for g in range(blocks):
        part = None
        for which, pull in enumerate((near, far)):
            spot = (1 - at[2] if which else at[2]) * half
            cols = pl.ds(pl.multiple_of(spot, half), half)
            extra = jnp.broadcast_to(sums[g, 0:1, cols], (EXTRA, half)).astype(BF16)
            lhs = jnp.concatenate([wide[g, :, cols], extra], axis=0)
            rhs = pull[g]
            wide_rhs = rhs.astype(F32)
            size = size + jnp.sum(wide_rhs * wide_rhs, axis=0, keepdims=True)
            product = jnp.dot(lhs, rhs, preferred_element_type=F32)
            part = product if part is None else part + product
        if g:
            total[...] += part
        else:
            total[...] = part
    grad[...] = finish(
        view[...],
        norm[...],
        vec[...],
        total[...],
        size * (0.5 / OFF_WEIGHT),
        1,
        6,
        images,
    )


def gradient(body, images, outs, name, at, wide, *operands):
    blocks, rows, width = wide.shape
    return pl.pallas_call(
        functools.partial(body, images),
        in_specs=[SMEM] + [VMEM] * (1 + len(operands)),
        out_specs=[VMEM] * len(outs),
        out_shape=outs,
        scratch_shapes=[pltpu.VMEM((rows + EXTRA, width), F32)],
        compiler_params=pltpu.CompilerParams(vmem_limit_bytes=24 * MIB),
        cost_estimate=pl.CostEstimate(
            flops=2 * rows * width * width * blocks,
            bytes_accessed=7 * MIB,
            transcendentals=0,
        ),
        name=name,
    )(at, wide, *operands)


def local(view_a, view_b):
    rows, width = view_a.shape
    chips = lax.axis_size("y") * lax.axis_size("x")
    blocks = lax.axis_size("z")
    images = rows * 2 * chips
    half = width // 2
    quarter = half // 4
    x_at, y_at, c_at, z_at = (lax.axis_index(name) for name in ("x", "y", "c", "z"))
    at = jnp.stack([x_at, y_at, c_at, z_at]).astype(jnp.int32)

    raw_b = lax.all_gather(view_b, "z", axis=0, tiled=False)
    late_a, raw_b = lax.optimization_barrier((view_a, raw_b))
    raw_a = lax.all_gather(late_a, "z", axis=0, tiled=False)
    swapped_b = swap(raw_b)

    values_a = view_a.astype(F32)
    values_b = view_b.astype(F32)
    local_a = jnp.sum(values_a, axis=0) / rows
    local_b = jnp.sum(values_b, axis=0) / rows
    apart_a = values_a - local_a
    apart_b = values_b - local_b
    mine = jnp.stack(
        [
            local_a,
            local_b,
            jnp.sum(apart_a * apart_a, axis=0),
            jnp.sum(apart_b * apart_b, axis=0),
            jnp.sum(apart_a * apart_b, axis=0),
        ]
    )
    pair = swap(mine)
    gap = mine[:2] - pair[:2]
    joined = jnp.concatenate(
        [
            (mine[:2] + pair[:2]) * 0.5,
            mine[2:4] + pair[2:4] + gap * gap * (rows / 2),
            mine[4:] + pair[4:] + gap[:1] * gap[1:] * (rows / 2),
        ]
    )
    all_stats = spread(joined, PLANE, chips)
    means = jnp.sum(all_stats[:, :2], axis=0) / chips
    away = all_stats[:, :2] - means
    squares = jnp.sum(all_stats[:, 2:4] + 2 * rows * away * away, axis=0)
    cross = jnp.sum(all_stats[:, 4] + 2 * rows * away[:, 0] * away[:, 1], axis=0)
    inverse = lax.rsqrt(squares / images + EPSILON)
    on_diagonal = cross / images * inverse[0] * inverse[1]
    deficit = 1.0 - on_diagonal
    pull_diagonal = lax.reduce_precision(-2.0 * deficit, 8, 7)
    norm_a = normalise(view_a, means[0], inverse[0])
    norm_b = normalise(view_b, means[1], inverse[1])

    stats = jnp.concatenate([means, inverse])
    wide_stats = spread(stats, "z", blocks)

    keep = lax.dynamic_slice_in_dim(norm_a, c_at * half, half, axis=1)
    give = lax.dynamic_slice_in_dim(norm_a, (1 - c_at) * half, half, axis=1)
    chip_a = jnp.concatenate([keep, swap(give)], axis=0).T.reshape(4, quarter, 2 * rows)
    lhs_x = rotate(chip_a, x_at).reshape(half, 2 * rows)
    lhs_y = rotate(chip_a, y_at).reshape(half, 2 * rows)

    wide_b, *parts = correlate(wide_stats, raw_b, swapped_b, lhs_x, lhs_y)

    def reduce(part, axis):
        total = part[0].astype(F32)
        for step in (1, 3, 2):
            total = total + shift(part[step], axis, step).astype(F32)
        return total.astype(BF16)

    first_0 = reduce(parts[:4], "x")
    first_1 = reduce(parts[4:], "y")
    pull_0, pull_1, outward = make_tile(
        at,
        2.0 * OFF_WEIGHT / images,
        [first_0] + others(first_0, "y"),
        [first_1] + others(first_1, "x"),
    )

    inward = lax.all_to_all(outward, "z", split_axis=0, concat_axis=0, tiled=True)

    def turned(piece, axis):
        ahead, behind, across = others(piece, axis)
        return [behind, across, ahead]

    shape = (blocks, half, width)
    row_pieces = [pull_0] + turned(pull_0, "x") + [pull_1] + turned(pull_1, "y")
    near_rows = pack(pack_rows_body, at, shape, "pack_rows", *row_pieces)
    col_pieces = turned(inward[:, 0], "x") + turned(inward[:, 1], "y")
    near_cols = pack(pack_cols_body, at, shape, "pack_cols", inward, *col_pieces)
    far_rows = swap(near_rows)
    far_cols = swap(near_cols)

    left = jnp.stack([jnp.sum(norm_a.astype(F32), axis=0), jnp.sum(norm_b.astype(F32), axis=0)])
    left, _ = lax.optimization_barrier((left, parts[7]))
    left = jnp.sum(spread(left + swap(left), PLANE, chips), axis=0)
    wide_left = spread(left, "z", blocks)
    wide_a = normalise(raw_a, wide_stats[:, 0:1], wide_stats[:, 2:3])

    vec = jnp.concatenate([stats, pull_diagonal[None], on_diagonal[None], left])
    grad_shape = jax.ShapeDtypeStruct(view_a.shape, BF16)
    grad_a, weight = gradient(
        rows_body,
        images,
        [grad_shape, jax.ShapeDtypeStruct((8, width), F32)],
        "rows",
        at,
        wide_b,
        wide_left,
        near_rows,
        far_rows,
        view_a,
        norm_b,
        vec,
    )
    share = jnp.sum(0.5 * weight[0] + deficit * deficit)
    loss_value = jnp.sum(spread(jnp.full((1, 128), share), "z", blocks)[:, 0, 0])
    (grad_b,) = gradient(
        cols_body,
        images,
        [grad_shape],
        "cols",
        at,
        wide_a,
        wide_left,
        near_cols,
        far_cols,
        view_b,
        norm_a,
        vec,
    )
    return (grad_a, grad_b, loss_value)


def solution(mesh):
    split = P(("y", "x", "c"), "z")
    chips = Mesh(mesh.devices.reshape(4, 4, 2, 8), ("y", "x", "c", "z"))
    return jax.shard_map(
        local,
        mesh=chips,
        in_specs=(split, split),
        out_specs=(split, split, P()),
        check_vma=False,
    )
```

```python
import functools

import jax
import jax.numpy as jnp
from jax import lax
from jax.experimental import pallas as pl
from jax.experimental.pallas import tpu as pltpu
from jax.sharding import Mesh, PartitionSpec as P

OFF_WEIGHT = 0.0051
EPSILON = 1e-05
F32 = jnp.float32
BF16 = jnp.bfloat16
PLANE = ("y", "x")
CONTRACT_LAST = (((1,), (1,)), ((), ()))
EXTRA = 16
MIB = 1 << 20
VMEM = pl.BlockSpec(memory_space=pltpu.VMEM)
SMEM = pl.BlockSpec(memory_space=pltpu.SMEM)


def shift(value, step, second=False):
    y_size, x_size = lax.axis_size("y"), lax.axis_size("x")
    pairs = []
    for y in range(y_size):
        for x in range(x_size):
            for c in range(2):
                along_y = (c == 1) != second
                to_y = (y + step) % y_size if along_y else y
                to_x = x if along_y else (x + step) % x_size
                pairs.append(((y * x_size + x) * 2 + c, (to_y * x_size + to_x) * 2 + c))
    return lax.ppermute(value, ("y", "x", "c"), pairs)


def swap(value):
    return lax.ppermute(value, "c", [(0, 1), (1, 0)])


def spread(value, axes, size):
    copies = jnp.broadcast_to(value[None], (size,) + value.shape)
    return lax.all_to_all(copies, axes, split_axis=0, concat_axis=0, tiled=True)


def rotate(value, by):
    twice = jnp.concatenate([value, value], axis=0)
    return lax.dynamic_slice_in_dim(twice, by, value.shape[0], axis=0)


def others(value, second=False):
    return [shift(value, step, second) for step in (1, 3, 2)]


def normalise(raw, mean, inverse):
    return ((raw.astype(F32) - mean) * inverse).astype(BF16)


def widen_body(at, stats, raw, wide, give):
    blocks, _, width = raw.shape
    half = width // 2
    spot = pl.ds(pl.multiple_of((1 - at[2]) * half, half), half)
    for g in range(blocks):
        wide[g] = normalise(raw[g], stats[g, 1:2], stats[g, 3:4])
        give[g] = wide[g, :, spot]


def widen(at, stats, raw):
    blocks, rows, width = raw.shape
    return pl.pallas_call(
        widen_body,
        in_specs=[SMEM] + [VMEM] * 2,
        out_specs=[VMEM] * 2,
        out_shape=[
            jax.ShapeDtypeStruct(raw.shape, BF16),
            jax.ShapeDtypeStruct((blocks, rows, width // 2), BF16),
        ],
        compiler_params=pltpu.CompilerParams(vmem_limit_bytes=16 * MIB),
        cost_estimate=pl.CostEstimate(
            flops=6 * blocks * rows * width, bytes_accessed=5 * MIB, transcendentals=0
        ),
        name="widen",
    )(at, stats, raw)


def correlate_body(at, wide, other, lhs, *parts):
    blocks, rows, half = other.shape
    quarter = lhs.shape[0] // 4
    spot = pl.ds(pl.multiple_of(at[2] * half, half), half)
    for g in range(blocks):
        rhs = jnp.concatenate([wide[g, :, spot], other[g]], axis=0)
        for turned in range(4):
            part = jnp.dot(
                lhs[turned * quarter : (turned + 1) * quarter],
                rhs,
                preferred_element_type=F32,
            )
            parts[turned][:, g * half : (g + 1) * half] = part.astype(BF16)


def correlate(at, wide, other, lhs):
    blocks, rows, half = other.shape
    part = jax.ShapeDtypeStruct((lhs.shape[0] // 4, blocks * half), BF16)
    return pl.pallas_call(
        correlate_body,
        in_specs=[SMEM] + [VMEM] * 3,
        out_specs=[VMEM] * 4,
        out_shape=[part] * 4,
        compiler_params=pltpu.CompilerParams(vmem_limit_bytes=16 * MIB),
        cost_estimate=pl.CostEstimate(
            flops=8 * rows * half * half * blocks, bytes_accessed=6 * MIB, transcendentals=0
        ),
        name="correlate",
    )(at, wide, other, lhs)


def tile_body(scale, at, own, ahead, behind, across, pull, outward):
    blocks, quarter, half = outward.shape
    row = lax.broadcasted_iota(jnp.int32, (quarter, half), 0)
    col = lax.broadcasted_iota(jnp.int32, (quarter, half), 1)
    same = col + at[2] * half == row + at[4] * quarter
    for g in range(blocks):
        cols = slice(g * half, (g + 1) * half)
        total = (own[:, cols].astype(F32) + across[:, cols].astype(F32)) + (
            ahead[:, cols].astype(F32) + behind[:, cols].astype(F32)
        )
        value = jnp.where(same & (at[3] == g), 0.0, scale * total).astype(BF16)
        pull[:, cols] = value
        outward[g] = value


def make_tile(at, scale, pieces, half):
    quarter, wide = pieces[0].shape
    return pl.pallas_call(
        functools.partial(tile_body, scale),
        in_specs=[SMEM] + [VMEM] * 4,
        out_specs=[VMEM] * 2,
        out_shape=[
            jax.ShapeDtypeStruct((quarter, wide), BF16),
            jax.ShapeDtypeStruct((wide // half, quarter, half), BF16),
        ],
        compiler_params=pltpu.CompilerParams(vmem_limit_bytes=16 * MIB),
        cost_estimate=pl.CostEstimate(
            flops=6 * quarter * wide, bytes_accessed=3 * MIB, transcendentals=0
        ),
        name="tile",
    )(at, *pieces)


def place(at, turned, quarter):
    spot = lax.rem(at[4] + turned, 4) * quarter
    return pl.ds(pl.multiple_of(spot, quarter), quarter)


def pack_body(at, *refs):
    pieces, out = refs[:4], refs[4]
    blocks, width, half = out.shape
    for turned in range(4):
        rows = place(at, turned, width // 4)
        for g in range(blocks):
            out[g, rows] = pieces[turned][:, g * half : (g + 1) * half]


def pack(at, pieces, half):
    quarter, wide = pieces[0].shape
    return pl.pallas_call(
        pack_body,
        in_specs=[SMEM] + [VMEM] * 4,
        out_specs=VMEM,
        out_shape=jax.ShapeDtypeStruct((wide // half, 4 * quarter, half), BF16),
        compiler_params=pltpu.CompilerParams(vmem_limit_bytes=16 * MIB),
        cost_estimate=pl.CostEstimate(flops=0, bytes_accessed=4 * MIB, transcendentals=0),
        name="pack",
    )(at, *pieces)


def finish(view, norm, vec, total, extra, weight, mean_row, left_row, images):
    mean, inverse = vec[mean_row : mean_row + 1], vec[mean_row + 2 : mean_row + 3]
    pull, match, left = vec[4:5], vec[5:6], vec[left_row : left_row + 1]
    back = total + norm.astype(F32) * pull
    centre = (extra + pull * left) * (1.0 / images)
    along = weight + pull * match
    white = (view.astype(F32) - mean) * inverse
    return (inverse * (back - centre - white * along)).astype(BF16)


def rows_body(images, at, wide, stats, near, far, view, norm, vec, grad, weight, total):
    blocks, rows, width = wide.shape
    half = width // 2
    ones = jnp.ones((EXTRA, half), BF16)
    sizes = [jnp.zeros((8, width), F32)] * 2
    for g in range(blocks):
        part = None
        for which, pull in enumerate((near, far)):
            spot = 1 - at[2] if which else at[2]
            cols = pl.ds(pl.multiple_of(spot * half, half), half)
            extra = jnp.broadcast_to(stats[g, 5:6, cols], (EXTRA, half)).astype(BF16)
            lhs = jnp.concatenate([wide[g, :, cols], extra], axis=0)
            rhs = pull[g]
            square = rhs.astype(F32)
            square = (square * square).astype(BF16)
            sizes[which] = sizes[which] + lax.dot_general(
                ones, square, CONTRACT_LAST, preferred_element_type=F32
            )[:8]
            product = lax.dot_general(lhs, rhs, CONTRACT_LAST, preferred_element_type=F32)
            part = product if part is None else part + product
        if g:
            total[...] += part
        else:
            total[...] = part
    size = (sizes[0] + sizes[1]) * (0.5 / OFF_WEIGHT)
    weight[...] = size
    grad[...] = finish(
        view[...], norm[...], vec[...], total[:rows], total[rows : rows + 1], size[0:1], 0, 7, images
    )


def cols_body(images, at, near, far, stats, view, norm, vec, *refs):
    pieces, (near_grad, far_grad, packed, total) = refs[:4], refs[4:]
    blocks, rows, width = near.shape
    half = width // 2
    spot = pl.ds(pl.multiple_of(at[2] * half, half), half)
    size = jnp.zeros((1, half), F32)
    for g in range(blocks):
        for turned in range(4):
            packed[g, place(at, turned, width // 4)] = pieces[turned][g]
        rhs = packed[g]
        square = rhs.astype(F32)
        size = size + jnp.sum(square * square, axis=0, keepdims=True)
        extra = jnp.broadcast_to(stats[g, 4:5], (EXTRA, width)).astype(BF16)
        lhs = jnp.concatenate([near[g], far[g], extra], axis=0)
        part = jnp.dot(lhs, rhs, preferred_element_type=F32)
        if g:
            total[...] += part
        else:
            total[...] = part
    weight = size * (0.5 / OFF_WEIGHT)
    for which, grad in enumerate((near_grad, far_grad)):
        part = slice(which * rows, (which + 1) * rows)
        grad[...] = finish(
            view[part, spot],
            norm[part, spot],
            vec[:, spot],
            total[part],
            total[2 * rows : 2 * rows + 1],
            weight,
            1,
            6,
            images,
        )


def gradient(body, images, outs, scratch, name, at, *operands):
    blocks, rows, width = operands[0].shape
    return pl.pallas_call(
        functools.partial(body, images),
        in_specs=[SMEM] + [VMEM] * len(operands),
        out_specs=[VMEM] * len(outs),
        out_shape=outs,
        scratch_shapes=scratch,
        compiler_params=pltpu.CompilerParams(vmem_limit_bytes=24 * MIB),
        cost_estimate=pl.CostEstimate(
            flops=2 * rows * width * width * blocks,
            bytes_accessed=7 * MIB,
            transcendentals=0,
        ),
        name=name,
    )(at, *operands)


def local(view_a, view_b):
    rows, width = view_a.shape
    chips = lax.axis_size("y") * lax.axis_size("x")
    blocks = lax.axis_size("z")
    images = rows * 2 * chips
    half = width // 2
    x_at, y_at, c_at, z_at = (lax.axis_index(name) for name in ("x", "y", "c", "z"))
    first_at = jnp.where(c_at == 0, x_at, y_at)
    at = jnp.stack([x_at, y_at, c_at, z_at, first_at]).astype(jnp.int32)

    raw_b = lax.all_gather(view_b, "z", axis=0, tiled=False)
    raw_a = lax.all_gather(view_a, "z", axis=0, tiled=False)
    chip_view = jnp.concatenate([view_b, swap(view_b)], axis=0)

    values_a = view_a.astype(F32)
    values_b = view_b.astype(F32)
    local_a = jnp.sum(values_a, axis=0) / rows
    local_b = jnp.sum(values_b, axis=0) / rows
    apart_a = values_a - local_a
    apart_b = values_b - local_b
    mine = jnp.stack(
        [
            local_a,
            local_b,
            jnp.sum(apart_a * apart_a, axis=0),
            jnp.sum(apart_b * apart_b, axis=0),
            jnp.sum(apart_a * apart_b, axis=0),
        ]
    )
    pair = swap(mine)
    gap = mine[:2] - pair[:2]
    joined = jnp.concatenate(
        [
            (mine[:2] + pair[:2]) * 0.5,
            mine[2:4] + pair[2:4] + gap * gap * (rows / 2),
            mine[4:] + pair[4:] + gap[:1] * gap[1:] * (rows / 2),
        ]
    )
    all_stats = spread(joined, PLANE, chips)
    means = jnp.sum(all_stats[:, :2], axis=0) / chips
    away = all_stats[:, :2] - means
    squares = jnp.sum(all_stats[:, 2:4] + 2 * rows * away * away, axis=0)
    cross = jnp.sum(all_stats[:, 4] + 2 * rows * away[:, 0] * away[:, 1], axis=0)
    inverse = lax.rsqrt(squares / images + EPSILON)
    on_diagonal = cross / images * inverse[0] * inverse[1]
    deficit = 1.0 - on_diagonal
    pull_diagonal = lax.reduce_precision(-2.0 * deficit, 8, 7)
    norm_a = normalise(view_a, means[0], inverse[0])
    norm_b = normalise(view_b, means[1], inverse[1])

    left = inverse * (2 * rows * jnp.sum(all_stats[:, :2], axis=0) - images * means)
    stats = jnp.concatenate([means, inverse, left])
    wide_stats = spread(stats, "z", blocks)

    chip_a = jnp.concatenate([norm_a, swap(norm_a)], axis=0)
    lhs = rotate(chip_a.T.reshape(4, width // 4, 2 * rows), first_at).reshape(width, 2 * rows)

    raw_b, wide_stats = lax.optimization_barrier((raw_b, wide_stats))
    wide_b, give = widen(at, wide_stats, raw_b)
    parts = correlate(at, wide_b, swap(give), lhs)
    total = parts[0].astype(F32)
    for step in (1, 3, 2):
        total = total + shift(parts[step], step).astype(F32)
    total = total.astype(BF16)
    pull, outward = make_tile(
        at, 2.0 * OFF_WEIGHT / images, [total] + others(total, second=True), half
    )
    inward = lax.all_to_all(outward, "z", split_axis=0, concat_axis=0, tiled=True)

    ahead, behind, across = others(pull)
    near_rows = pack(at, [pull, behind, across, ahead], half)
    far_rows = swap(near_rows)
    ahead, behind, across = others(inward)
    col_pieces = [inward, behind, across, ahead]

    wide_a = normalise(raw_a, wide_stats[:, 0:1], wide_stats[:, 2:3])
    far_a = swap(wide_a)

    vec = jnp.concatenate([stats[:4], pull_diagonal[None], on_diagonal[None], left])
    grad_a, weight = gradient(
        rows_body,
        images,
        [jax.ShapeDtypeStruct(view_a.shape, BF16), jax.ShapeDtypeStruct((8, width), F32)],
        [pltpu.VMEM((rows + EXTRA, width), F32)],
        "rows",
        at,
        wide_b,
        wide_stats,
        near_rows,
        far_rows,
        view_a,
        norm_b,
        vec,
    )
    share = jnp.sum(0.5 * weight[0] + deficit * deficit)
    loss_value = jnp.sum(spread(jnp.full((1, 128), share), "z", blocks)[:, 0, 0])
    near_grad, far_grad = gradient(
        cols_body,
        images,
        [jax.ShapeDtypeStruct((rows, half), BF16)] * 2,
        [pltpu.VMEM((blocks, width, half), BF16), pltpu.VMEM((2 * rows + EXTRA, half), F32)],
        "cols",
        at,
        wide_a,
        far_a,
        wide_stats,
        chip_view,
        chip_a,
        vec,
        *col_pieces,
    )
    other_grad = swap(far_grad)
    grad_b = jnp.where(
        c_at == 0,
        jnp.concatenate([near_grad, other_grad], axis=1),
        jnp.concatenate([other_grad, near_grad], axis=1),
    )
    return (grad_a, grad_b, loss_value)


def solution(mesh):
    split = P(("y", "x", "c"), "z")
    chips = Mesh(mesh.devices.reshape(4, 4, 2, 8), ("y", "x", "c", "z"))
    return jax.shard_map(
        local,
        mesh=chips,
        in_specs=(split, split),
        out_specs=(split, split, P()),
        check_vma=False,
    )
```

```python
import functools

import jax
import jax.numpy as jnp
from jax import lax
from jax.experimental import pallas as pl
from jax.experimental.pallas import tpu as pltpu
from jax.sharding import Mesh, PartitionSpec as P

OFF_WEIGHT = 0.0051
EPSILON = 1e-05
F32 = jnp.float32
BF16 = jnp.bfloat16
PLANE = ("y", "x")
CONTRACT_LAST = (((1,), (1,)), ((), ()))
EXTRA = 16
MIB = 1 << 20
VMEM = pl.BlockSpec(memory_space=pltpu.VMEM)
SMEM = pl.BlockSpec(memory_space=pltpu.SMEM)


def shift(value, step, second=False):
    y_size, x_size = lax.axis_size("y"), lax.axis_size("x")
    pairs = []
    for y in range(y_size):
        for x in range(x_size):
            for c in range(2):
                along_y = (c == 1) != second
                to_y = (y + step) % y_size if along_y else y
                to_x = x if along_y else (x + step) % x_size
                pairs.append(((y * x_size + x) * 2 + c, (to_y * x_size + to_x) * 2 + c))
    return lax.ppermute(value, ("y", "x", "c"), pairs)


def swap(value):
    return lax.ppermute(value, "c", [(0, 1), (1, 0)])


def spread(value, axes, size):
    copies = jnp.broadcast_to(value[None], (size,) + value.shape)
    return lax.all_to_all(copies, axes, split_axis=0, concat_axis=0, tiled=True)


def rotate(value, by):
    twice = jnp.concatenate([value, value], axis=0)
    return lax.dynamic_slice_in_dim(twice, by, value.shape[0], axis=0)


def others(value, second=False):
    return [shift(value, step, second) for step in (1, 3, 2)]


def normalise(raw, mean, inverse):
    return ((raw.astype(F32) - mean) * inverse).astype(BF16)


def widen_body(at, stats, raw, keep, give):
    blocks, _, half = keep.shape
    for place, out in enumerate((keep, give)):
        spot = 1 - at[2] if place else at[2]
        cols = pl.ds(pl.multiple_of(spot * half, half), half)
        for g in range(blocks):
            out[g] = normalise(raw[g, :, cols], stats[g, 1:2, cols], stats[g, 3:4, cols])


def widen(at, stats, raw):
    blocks, rows, width = raw.shape
    return pl.pallas_call(
        widen_body,
        in_specs=[SMEM] + [VMEM] * 2,
        out_specs=[VMEM] * 2,
        out_shape=[jax.ShapeDtypeStruct((blocks, rows, width // 2), BF16)] * 2,
        compiler_params=pltpu.CompilerParams(vmem_limit_bytes=16 * MIB),
        cost_estimate=pl.CostEstimate(
            flops=6 * blocks * rows * width, bytes_accessed=4 * MIB, transcendentals=0
        ),
        name="widen",
    )(at, stats, raw)


def correlate_body(keep, other, lhs, *parts):
    blocks, rows, half = other.shape
    quarter = lhs.shape[0] // 4
    for g in range(blocks):
        rhs = jnp.concatenate([keep[g], other[g]], axis=0)
        for turned in range(4):
            part = jnp.dot(
                lhs[turned * quarter : (turned + 1) * quarter],
                rhs,
                preferred_element_type=F32,
            )
            parts[turned][g] = part.astype(BF16)


def correlate(keep, other, lhs):
    blocks, rows, half = other.shape
    part = jax.ShapeDtypeStruct((blocks, lhs.shape[0] // 4, half), BF16)
    return pl.pallas_call(
        correlate_body,
        in_specs=[VMEM] * 3,
        out_specs=[VMEM] * 4,
        out_shape=[part] * 4,
        compiler_params=pltpu.CompilerParams(vmem_limit_bytes=16 * MIB),
        cost_estimate=pl.CostEstimate(
            flops=8 * rows * half * half * blocks, bytes_accessed=4 * MIB, transcendentals=0
        ),
        name="correlate",
    )(keep, other, lhs)


def tile_body(scale, at, diagonal, own, ahead, behind, across, pull, outward):
    blocks, quarter, half = pull.shape
    row = lax.broadcasted_iota(jnp.int32, (quarter, half), 0)
    col = lax.broadcasted_iota(jnp.int32, (quarter, half), 1)
    same = col + at[2] * half == row + at[4] * quarter
    size = jnp.zeros((8, half), F32)
    for g in range(blocks):
        total = (own[g].astype(F32) + across[g].astype(F32)) + (
            ahead[g].astype(F32) + behind[g].astype(F32)
        )
        value = jnp.where(same & (at[3] == g), 0.0, scale * total).astype(BF16)
        pull[g] = value
        outward[g, :quarter] = value
        wide = value.astype(F32)
        size = size + jnp.sum((wide * wide).reshape(quarter // 8, 8, half), axis=0)
    share = diagonal[0:1, 0:1] + (0.25 / OFF_WEIGHT) * jnp.sum(size).reshape(1, 1)
    share = jnp.broadcast_to(share, (EXTRA, half))
    high = share.astype(BF16)
    share = share - high.astype(F32)
    middle = share.astype(BF16)
    low = (share - middle.astype(F32)).astype(BF16)
    line = lax.broadcasted_iota(jnp.int32, (EXTRA, half), 0)
    extra = jnp.where(line == 0, high, jnp.where(line == 1, middle, low))
    for g in range(blocks):
        outward[g, quarter:] = extra


def make_tile(at, scale, diagonal, pieces):
    blocks, quarter, half = pieces[0].shape
    return pl.pallas_call(
        functools.partial(tile_body, scale),
        in_specs=[SMEM] + [VMEM] * 5,
        out_specs=[VMEM] * 2,
        out_shape=[
            jax.ShapeDtypeStruct(pieces[0].shape, BF16),
            jax.ShapeDtypeStruct((blocks, quarter + EXTRA, half), BF16),
        ],
        compiler_params=pltpu.CompilerParams(vmem_limit_bytes=16 * MIB),
        cost_estimate=pl.CostEstimate(
            flops=6 * pieces[0].size, bytes_accessed=3 * MIB, transcendentals=0
        ),
        name="tile",
    )(at, diagonal, *pieces)


def place(at, turned, quarter):
    spot = lax.rem(at[4] + turned, 4) * quarter
    return pl.ds(pl.multiple_of(spot, quarter), quarter)


def finish(view, norm, vec, total, extra, weight, mean_row, left_row, images):
    mean, inverse = vec[mean_row : mean_row + 1], vec[mean_row + 2 : mean_row + 3]
    pull, match, left = vec[4:5], vec[5:6], vec[left_row : left_row + 1]
    back = total + norm.astype(F32) * pull
    centre = (extra + pull * left) * (1.0 / images)
    along = weight + pull * match
    white = (view.astype(F32) - mean) * inverse
    return (inverse * (back - centre - white * along)).astype(BF16)


def rows_body(at, near, far, stats, *refs):
    pieces, (near_part, far_part, packed) = refs[:4], refs[4:]
    blocks, rows, half = near.shape
    width = 2 * half
    cols = pl.ds(pl.multiple_of(at[2] * half, half), half)
    ones = jnp.ones((EXTRA, half), BF16)
    size = jnp.zeros((EXTRA, width), F32)
    for g in range(blocks):
        for turned in range(4):
            packed[place(at, turned, width // 4)] = pieces[turned][g]
        rhs = packed[...]
        square = rhs.astype(F32)
        square = (square * square).astype(BF16)
        size = size + lax.dot_general(
            ones, square, CONTRACT_LAST, preferred_element_type=F32
        )
        extra = jnp.broadcast_to(stats[g, 5:6, cols], (EXTRA, half)).astype(BF16)
        lhs = jnp.concatenate([far[g], extra], axis=0)
        far_more = lax.dot_general(lhs, rhs, CONTRACT_LAST, preferred_element_type=F32)
        near_more = lax.dot_general(
            near[g], rhs, CONTRACT_LAST, preferred_element_type=F32
        )
        if g:
            far_part[: rows + EXTRA] += far_more
            near_part[:rows] += near_more
        else:
            far_part[: rows + EXTRA] = far_more
            near_part[:rows] = near_more
    far_part[rows + 8 : rows + EXTRA] = size[:8] * (0.5 / OFF_WEIGHT)
    near_part[rows:] = far_part[rows:]


def cols_body(images, at, near, far, stats, view, norm, vec, *refs):
    pieces, (near_grad, far_grad, loss, packed, total) = refs[:4], refs[4:]
    blocks, rows, width = near.shape
    half = width // 2
    spot = pl.ds(pl.multiple_of(at[2] * half, half), half)
    size = jnp.zeros((1, half), F32)
    for g in range(blocks):
        for turned in range(4):
            packed[g, place(at, turned, width // 4)] = pieces[turned][g, : width // 4]
        rhs = packed[g]
        square = rhs.astype(F32)
        size = size + jnp.sum(square * square, axis=0, keepdims=True)
        extra = jnp.broadcast_to(stats[g, 4:5], (EXTRA, width)).astype(BF16)
        lhs = jnp.concatenate([near[g], far[g], extra], axis=0)
        part = jnp.dot(lhs, rhs, preferred_element_type=F32)
        if g:
            total[...] += part
        else:
            total[...] = part
    shares = []
    for turned in range(4):
        share = jnp.zeros((1, 128), F32)
        for g in range(blocks):
            lines = pieces[turned][g, width // 4 :, :128].astype(F32)
            share = share + ((lines[0:1] + lines[1:2]) + lines[2:3])
        shares.append(share)
    loss[...] = (shares[0] + shares[2]) + (shares[1] + shares[3])
    weight = size * (0.5 / OFF_WEIGHT)
    for which, grad in enumerate((near_grad, far_grad)):
        part = slice(which * rows, (which + 1) * rows)
        grad[...] = finish(
            view[part, spot],
            norm[part, spot],
            vec[:, spot],
            total[part],
            total[2 * rows : 2 * rows + 1],
            weight,
            1,
            6,
            images,
        )


def gradient(body, outs, scratch, name, *operands):
    return pl.pallas_call(
        body,
        in_specs=[SMEM] + [VMEM] * (len(operands) - 1),
        out_specs=[VMEM] * len(outs),
        out_shape=outs,
        scratch_shapes=scratch,
        compiler_params=pltpu.CompilerParams(vmem_limit_bytes=24 * MIB),
        cost_estimate=pl.CostEstimate(
            flops=1, bytes_accessed=1, transcendentals=0
        ),
        name=name,
    )(*operands)


def local(view_a, view_b):
    rows, width = view_a.shape
    chips = lax.axis_size("y") * lax.axis_size("x")
    blocks = lax.axis_size("z")
    images = rows * 2 * chips
    half = width // 2
    x_at, y_at, c_at, z_at = (lax.axis_index(name) for name in ("x", "y", "c", "z"))
    first_at = jnp.where(c_at == 0, x_at, y_at)
    at = jnp.stack([x_at, y_at, c_at, z_at, first_at]).astype(jnp.int32)

    raw_b = lax.all_gather(view_b, "z", axis=0, tiled=False)
    raw_a = lax.all_gather(view_a, "z", axis=0, tiled=False)
    chip_view = jnp.concatenate([view_b, swap(view_b)], axis=0)

    values_a = view_a.astype(F32)
    values_b = view_b.astype(F32)
    local_a = jnp.sum(values_a, axis=0) / rows
    local_b = jnp.sum(values_b, axis=0) / rows
    apart_a = values_a - local_a
    apart_b = values_b - local_b
    mine = jnp.stack(
        [
            local_a,
            local_b,
            jnp.sum(apart_a * apart_a, axis=0),
            jnp.sum(apart_b * apart_b, axis=0),
            jnp.sum(apart_a * apart_b, axis=0),
        ]
    )
    pair = swap(mine)
    gap = mine[:2] - pair[:2]
    joined = jnp.concatenate(
        [
            (mine[:2] + pair[:2]) * 0.5,
            mine[2:4] + pair[2:4] + gap * gap * (rows / 2),
            mine[4:] + pair[4:] + gap[:1] * gap[1:] * (rows / 2),
        ]
    )
    all_stats = spread(joined, PLANE, chips)
    means = jnp.sum(all_stats[:, :2], axis=0) / chips
    away = all_stats[:, :2] - means
    squares = jnp.sum(all_stats[:, 2:4] + 2 * rows * away * away, axis=0)
    cross = jnp.sum(all_stats[:, 4] + 2 * rows * away[:, 0] * away[:, 1], axis=0)
    inverse = lax.rsqrt(squares / images + EPSILON)
    on_diagonal = cross / images * inverse[0] * inverse[1]
    deficit = 1.0 - on_diagonal
    pull_diagonal = lax.reduce_precision(-2.0 * deficit, 8, 7)
    norm_a = normalise(view_a, means[0], inverse[0])
    norm_b = normalise(view_b, means[1], inverse[1])

    left = inverse * (2 * rows * jnp.sum(all_stats[:, :2], axis=0) - images * means)
    stats = jnp.concatenate([means, inverse, left])
    wide_stats = spread(stats, "z", blocks)
    vec = jnp.concatenate([stats[:4], pull_diagonal[None], on_diagonal[None], left])

    chip_a = jnp.concatenate([norm_a, swap(norm_a)], axis=0)
    lhs = rotate(chip_a.T.reshape(4, width // 4, 2 * rows), first_at).reshape(width, 2 * rows)

    raw_b, wide_stats, lhs, chip_a, chip_view, vec = lax.optimization_barrier(
        (raw_b, wide_stats, lhs, chip_a, chip_view, vec)
    )
    near_b, give = widen(at, wide_stats, raw_b)
    far_b = swap(give)
    parts = correlate(near_b, far_b, lhs)
    total = parts[0].astype(F32)
    for step in (1, 3, 2):
        total = total + shift(parts[step], step).astype(F32)
    total = total.astype(BF16)
    diagonal = jnp.sum((deficit * deficit).reshape(4, width // 4), axis=1)
    diagonal = 0.5 * lax.dynamic_slice_in_dim(diagonal, first_at, 1, axis=0)
    diagonal = jnp.broadcast_to(diagonal[None], (1, 128))
    pull, outward = make_tile(
        at, 2.0 * OFF_WEIGHT / images, diagonal, [total] + others(total, second=True)
    )
    inward = lax.all_to_all(outward, "z", split_axis=0, concat_axis=0, tiled=True)

    ahead, behind, across = others(pull)
    row_pieces = [pull, behind, across, ahead]
    row_pieces, inward, raw_a = lax.optimization_barrier((row_pieces, inward, raw_a))
    ahead, behind, across = others(inward)
    col_pieces = [inward, behind, across, ahead]
    row_pieces, col_pieces = lax.optimization_barrier((row_pieces, col_pieces))

    wide_a = normalise(raw_a, wide_stats[:, 0:1], wide_stats[:, 2:3])
    far_a = swap(wide_a)

    part = jax.ShapeDtypeStruct((rows + EXTRA, width), F32)
    near_part, far_part = gradient(
        rows_body,
        [part, part],
        [pltpu.VMEM((width, half), BF16)],
        "rows",
        at,
        near_b,
        far_b,
        wide_stats,
        *row_pieces,
    )
    far_a, far_part = lax.optimization_barrier((far_a, far_part))
    near_part = near_part + swap(far_part)
    grad_a = finish(
        view_a,
        norm_b,
        vec,
        near_part[:rows],
        near_part[rows : rows + 1],
        near_part[rows + 8 : rows + 9],
        0,
        7,
        images,
    )
    near_grad, far_grad, loss = gradient(
        functools.partial(cols_body, images),
        [jax.ShapeDtypeStruct((rows, half), BF16)] * 2 + [jax.ShapeDtypeStruct((1, 128), F32)],
        [pltpu.VMEM((blocks, width, half), BF16), pltpu.VMEM((2 * rows + EXTRA, half), F32)],
        "cols",
        at,
        wide_a,
        far_a,
        wide_stats,
        chip_view,
        chip_a,
        vec,
        *col_pieces,
    )
    loss_value = (loss + swap(loss))[0, 0]
    other_grad = swap(far_grad)
    grad_b = jnp.where(
        c_at == 0,
        jnp.concatenate([near_grad, other_grad], axis=1),
        jnp.concatenate([other_grad, near_grad], axis=1),
    )
    return (grad_a, grad_b, loss_value)


def solution(mesh):
    split = P(("y", "x", "c"), "z")
    chips = Mesh(mesh.devices.reshape(4, 4, 2, 8), ("y", "x", "c", "z"))
    return jax.shard_map(
        local,
        mesh=chips,
        in_specs=(split, split),
        out_specs=(split, split, P()),
        check_vma=False,
    )
```

```python
import functools

import jax
import jax.numpy as jnp
from jax import lax
from jax.experimental import pallas as pl
from jax.experimental.pallas import tpu as pltpu
from jax.sharding import Mesh, PartitionSpec as P

OFF_WEIGHT = 0.0051
EPSILON = 1e-05
F32 = jnp.float32
BF16 = jnp.bfloat16
PLANE = ("y", "x")
CONTRACT_LAST = (((1,), (1,)), ((), ()))
EXTRA = 16
MIB = 1 << 20
VMEM = pl.BlockSpec(memory_space=pltpu.VMEM)
SMEM = pl.BlockSpec(memory_space=pltpu.SMEM)


def shift(value, step, second=False):
    y_size, x_size = lax.axis_size("y"), lax.axis_size("x")
    pairs = []
    for y in range(y_size):
        for x in range(x_size):
            for c in range(2):
                along_y = (c == 1) != second
                to_y = (y + step) % y_size if along_y else y
                to_x = x if along_y else (x + step) % x_size
                pairs.append(((y * x_size + x) * 2 + c, (to_y * x_size + to_x) * 2 + c))
    return lax.ppermute(value, ("y", "x", "c"), pairs)


def swap(value):
    return lax.ppermute(value, "c", [(0, 1), (1, 0)])


def spread(value, axes, size):
    copies = jnp.broadcast_to(value[None], (size,) + value.shape)
    return lax.all_to_all(copies, axes, split_axis=0, concat_axis=0, tiled=True)


def rotate(value, by):
    twice = jnp.concatenate([value, value], axis=0)
    return lax.dynamic_slice_in_dim(twice, by, value.shape[0], axis=0)


def others(value, second=False):
    return [shift(value, step, second) for step in (1, 3, 2)]


def normalise(raw, mean, inverse):
    return ((raw.astype(F32) - mean) * inverse).astype(BF16)


def rounded(raw, mean, inverse):
    return lax.reduce_precision((raw.astype(F32) - mean) * inverse, 8, 7).astype(BF16)


def widen_body(at, stats, raw, keep, give):
    blocks, _, half = keep.shape
    for place, out in enumerate((keep, give)):
        spot = 1 - at[2] if place else at[2]
        cols = pl.ds(pl.multiple_of(spot * half, half), half)
        for g in range(blocks):
            out[g] = normalise(raw[g, :, cols], stats[g, 1:2, cols], stats[g, 3:4, cols])


def widen(at, stats, raw):
    blocks, rows, width = raw.shape
    return pl.pallas_call(
        widen_body,
        in_specs=[SMEM] + [VMEM] * 2,
        out_specs=[VMEM] * 2,
        out_shape=[jax.ShapeDtypeStruct((blocks, rows, width // 2), BF16)] * 2,
        compiler_params=pltpu.CompilerParams(vmem_limit_bytes=6 * MIB),
        cost_estimate=pl.CostEstimate(
            flops=6 * blocks * rows * width, bytes_accessed=4 * MIB, transcendentals=0
        ),
        name="widen",
    )(at, stats, raw)


def correlate_body(keep, other, lhs, *parts):
    blocks, rows, half = other.shape
    quarter = lhs.shape[0] // 4
    for g in range(blocks):
        rhs = jnp.concatenate([keep[g], other[g]], axis=0)
        for turned in range(4):
            part = jnp.dot(
                lhs[turned * quarter : (turned + 1) * quarter],
                rhs,
                preferred_element_type=F32,
            )
            parts[turned][g] = part.astype(BF16)


def correlate(keep, other, lhs):
    blocks, rows, half = other.shape
    part = jax.ShapeDtypeStruct((blocks, lhs.shape[0] // 4, half), BF16)
    return pl.pallas_call(
        correlate_body,
        in_specs=[VMEM] * 3,
        out_specs=[VMEM] * 4,
        out_shape=[part] * 4,
        compiler_params=pltpu.CompilerParams(vmem_limit_bytes=6 * MIB),
        cost_estimate=pl.CostEstimate(
            flops=8 * rows * half * half * blocks, bytes_accessed=4 * MIB, transcendentals=0
        ),
        name="correlate",
    )(keep, other, lhs)


def tile_body(scale, at, diagonal, own, ahead, behind, across, pull, outward):
    blocks, quarter, half = pull.shape
    row = lax.broadcasted_iota(jnp.int32, (quarter, half), 0)
    col = lax.broadcasted_iota(jnp.int32, (quarter, half), 1)
    same = col + at[2] * half == row + at[4] * quarter
    size = jnp.zeros((8, half), F32)
    for g in range(blocks):
        total = (own[g].astype(F32) + across[g].astype(F32)) + (
            ahead[g].astype(F32) + behind[g].astype(F32)
        )
        value = jnp.where(same & (at[3] == g), 0.0, scale * total).astype(BF16)
        pull[g] = value
        outward[g, :quarter] = value
        wide = value.astype(F32)
        size = size + jnp.sum((wide * wide).reshape(quarter // 8, 8, half), axis=0)
    share = diagonal[0:1, 0:1] + (0.25 / OFF_WEIGHT) * jnp.sum(size).reshape(1, 1)
    share = jnp.broadcast_to(share, (EXTRA, half))
    high = share.astype(BF16)
    share = share - high.astype(F32)
    middle = share.astype(BF16)
    low = (share - middle.astype(F32)).astype(BF16)
    line = lax.broadcasted_iota(jnp.int32, (EXTRA, half), 0)
    extra = jnp.where(line == 0, high, jnp.where(line == 1, middle, low))
    for g in range(blocks):
        outward[g, quarter:] = extra


def make_tile(at, scale, diagonal, pieces):
    blocks, quarter, half = pieces[0].shape
    return pl.pallas_call(
        functools.partial(tile_body, scale),
        in_specs=[SMEM] + [VMEM] * 5,
        out_specs=[VMEM] * 2,
        out_shape=[
            jax.ShapeDtypeStruct(pieces[0].shape, BF16),
            jax.ShapeDtypeStruct((blocks, quarter + EXTRA, half), BF16),
        ],
        compiler_params=pltpu.CompilerParams(vmem_limit_bytes=6 * MIB),
        cost_estimate=pl.CostEstimate(
            flops=6 * pieces[0].size, bytes_accessed=3 * MIB, transcendentals=0
        ),
        name="tile",
    )(at, diagonal, *pieces)


def place(at, turned, quarter):
    spot = lax.rem(at[4] + turned, 4) * quarter
    return pl.ds(pl.multiple_of(spot, quarter), quarter)


def finish(view, norm, vec, total, extra, weight, mean_row, left_row, images):
    mean, inverse = vec[mean_row : mean_row + 1], vec[mean_row + 2 : mean_row + 3]
    pull, match, left = vec[4:5], vec[5:6], vec[left_row : left_row + 1]
    back = total + norm.astype(F32) * pull
    centre = (extra + pull * left) * (1.0 / images)
    along = weight + pull * match
    white = (view.astype(F32) - mean) * inverse
    return (inverse * (back - centre - white * along)).astype(BF16)


def rows_body(at, near, far, stats, *refs):
    pieces, (near_part, far_part, packed) = refs[:4], refs[4:]
    blocks, rows, half = near.shape
    width = 2 * half
    cols = pl.ds(pl.multiple_of(at[2] * half, half), half)
    ones = jnp.ones((EXTRA, half), BF16)
    size = jnp.zeros((EXTRA, width), F32)
    for g in range(blocks):
        for turned in range(4):
            packed[place(at, turned, width // 4)] = pieces[turned][g]
        rhs = packed[...]
        square = rhs.astype(F32)
        square = (square * square).astype(BF16)
        size = size + lax.dot_general(
            ones, square, CONTRACT_LAST, preferred_element_type=F32
        )
        extra = jnp.broadcast_to(stats[g, 5:6, cols], (EXTRA, half)).astype(BF16)
        lhs = jnp.concatenate([far[g], extra], axis=0)
        far_more = lax.dot_general(lhs, rhs, CONTRACT_LAST, preferred_element_type=F32)
        near_more = lax.dot_general(
            near[g], rhs, CONTRACT_LAST, preferred_element_type=F32
        )
        if g:
            far_part[: rows + EXTRA] += far_more
            near_part[:rows] += near_more
        else:
            far_part[: rows + EXTRA] = far_more
            near_part[:rows] = near_more
    far_part[rows + 8 : rows + EXTRA] = size[:8] * (0.5 / OFF_WEIGHT)
    near_part[rows:] = far_part[rows:]


def cols_body(images, at, near, far, stats, view, norm, vec, *refs):
    pieces, (near_grad, far_grad, loss, packed, total) = refs[:4], refs[4:]
    blocks, rows, width = near.shape
    half = width // 2
    spot = pl.ds(pl.multiple_of(at[2] * half, half), half)
    size = jnp.zeros((1, half), F32)
    for g in range(blocks):
        for turned in range(4):
            packed[g, place(at, turned, width // 4)] = pieces[turned][g, : width // 4]
        rhs = packed[g]
        square = rhs.astype(F32)
        size = size + jnp.sum(square * square, axis=0, keepdims=True)
        extra = jnp.broadcast_to(stats[g, 4:5], (EXTRA, width)).astype(BF16)
        lhs = jnp.concatenate([near[g], far[g], extra], axis=0)
        part = jnp.dot(lhs, rhs, preferred_element_type=F32)
        if g:
            total[...] += part
        else:
            total[...] = part
    shares = []
    for turned in range(4):
        share = jnp.zeros((1, 128), F32)
        for g in range(blocks):
            lines = pieces[turned][g, width // 4 :, :128].astype(F32)
            share = share + ((lines[0:1] + lines[1:2]) + lines[2:3])
        shares.append(share)
    loss[...] = (shares[0] + shares[2]) + (shares[1] + shares[3])
    weight = size * (0.5 / OFF_WEIGHT)
    for which, grad in enumerate((near_grad, far_grad)):
        part = slice(which * rows, (which + 1) * rows)
        grad[...] = finish(
            view[part, spot],
            norm[part, spot],
            vec[:, spot],
            total[part],
            total[2 * rows : 2 * rows + 1],
            weight,
            1,
            6,
            images,
        )


def gradient(body, outs, scratch, name, *operands):
    return pl.pallas_call(
        body,
        in_specs=[SMEM] + [VMEM] * (len(operands) - 1),
        out_specs=[VMEM] * len(outs),
        out_shape=outs,
        scratch_shapes=scratch,
        compiler_params=pltpu.CompilerParams(vmem_limit_bytes=10 * MIB),
        cost_estimate=pl.CostEstimate(
            flops=1 << 30, bytes_accessed=7 * MIB, transcendentals=0
        ),
        name=name,
    )(*operands)


def local(view_a, view_b):
    rows, width = view_a.shape
    chips = lax.axis_size("y") * lax.axis_size("x")
    blocks = lax.axis_size("z")
    images = rows * 2 * chips
    half = width // 2
    x_at, y_at, c_at, z_at = (lax.axis_index(name) for name in ("x", "y", "c", "z"))
    first_at = jnp.where(c_at == 0, x_at, y_at)
    at = jnp.stack([x_at, y_at, c_at, z_at, first_at]).astype(jnp.int32)

    raw_b = lax.all_gather(view_b, "z", axis=0, tiled=False)
    raw_a = lax.all_gather(view_a, "z", axis=0, tiled=False)
    chip_view = jnp.concatenate([view_b, swap(view_b)], axis=0)

    values_a = view_a.astype(F32)
    values_b = view_b.astype(F32)
    local_a = jnp.sum(values_a, axis=0) / rows
    local_b = jnp.sum(values_b, axis=0) / rows
    apart_a = values_a - local_a
    apart_b = values_b - local_b
    mine = jnp.stack(
        [
            local_a,
            local_b,
            jnp.sum(apart_a * apart_a, axis=0),
            jnp.sum(apart_b * apart_b, axis=0),
            jnp.sum(apart_a * apart_b, axis=0),
        ]
    )
    pair = swap(mine)
    gap = mine[:2] - pair[:2]
    joined = jnp.concatenate(
        [
            (mine[:2] + pair[:2]) * 0.5,
            mine[2:4] + pair[2:4] + gap * gap * (rows / 2),
            mine[4:] + pair[4:] + gap[:1] * gap[1:] * (rows / 2),
        ]
    )
    all_stats = spread(joined, PLANE, chips)
    means = jnp.sum(all_stats[:, :2], axis=0) / chips
    away = all_stats[:, :2] - means
    squares = jnp.sum(all_stats[:, 2:4] + 2 * rows * away * away, axis=0)
    cross = jnp.sum(all_stats[:, 4] + 2 * rows * away[:, 0] * away[:, 1], axis=0)
    inverse = lax.rsqrt(squares / images + EPSILON)
    on_diagonal = cross / images * inverse[0] * inverse[1]
    deficit = 1.0 - on_diagonal
    pull_diagonal = lax.reduce_precision(-2.0 * deficit, 8, 7)
    norm_a = rounded(view_a, means[0], inverse[0])
    norm_b = rounded(view_b, means[1], inverse[1])

    left = inverse * (2 * rows * jnp.sum(all_stats[:, :2], axis=0) - images * means)
    stats = jnp.concatenate([means, inverse, left])
    wide_stats = spread(stats, "z", blocks)
    vec = jnp.concatenate([stats[:4], pull_diagonal[None], on_diagonal[None], left])

    chip_a = jnp.concatenate([norm_a, swap(norm_a)], axis=0)
    lhs = rotate(chip_a.T.reshape(4, width // 4, 2 * rows), first_at).reshape(width, 2 * rows)

    raw_b, wide_stats, lhs, chip_a, chip_view, vec = lax.optimization_barrier(
        (raw_b, wide_stats, lhs, chip_a, chip_view, vec)
    )
    near_b, give = widen(at, wide_stats, raw_b)
    far_b = swap(give)
    parts = correlate(near_b, far_b, lhs)
    total = parts[0].astype(F32)
    for step in (1, 3, 2):
        total = total + shift(parts[step], step).astype(F32)
    total = total.astype(BF16)
    diagonal = jnp.sum((deficit * deficit).reshape(4, width // 4), axis=1)
    diagonal = 0.5 * lax.dynamic_slice_in_dim(diagonal, first_at, 1, axis=0)
    diagonal = jnp.broadcast_to(diagonal[None], (1, 128))
    pull, outward = make_tile(
        at, 2.0 * OFF_WEIGHT / images, diagonal, [total] + others(total, second=True)
    )
    inward = lax.all_to_all(outward, "z", split_axis=0, concat_axis=0, tiled=True)

    ahead, behind, across = others(pull)
    row_pieces = [pull, behind, across, ahead]
    row_pieces, inward, raw_a = lax.optimization_barrier((row_pieces, inward, raw_a))
    ahead, behind, across = others(inward)
    col_pieces = [inward, behind, across, ahead]

    wide_a = rounded(raw_a, wide_stats[:, 0:1], wide_stats[:, 2:3])
    far_a = rounded(swap(raw_a), wide_stats[:, 0:1], wide_stats[:, 2:3])

    part = jax.ShapeDtypeStruct((rows + EXTRA, width), F32)
    near_part, far_part = gradient(
        rows_body,
        [part, part],
        [pltpu.VMEM((width, half), BF16)],
        "rows",
        at,
        near_b,
        far_b,
        wide_stats,
        *row_pieces,
    )
    far_a, far_part = lax.optimization_barrier((far_a, far_part))
    near_part = near_part + swap(far_part)
    grad_a = finish(
        view_a,
        norm_b,
        vec,
        near_part[:rows],
        near_part[rows : rows + 1],
        near_part[rows + 8 : rows + 9],
        0,
        7,
        images,
    )
    near_grad, far_grad, loss = gradient(
        functools.partial(cols_body, images),
        [jax.ShapeDtypeStruct((rows, half), BF16)] * 2 + [jax.ShapeDtypeStruct((1, 128), F32)],
        [pltpu.VMEM((blocks, width, half), BF16), pltpu.VMEM((2 * rows + EXTRA, half), F32)],
        "cols",
        at,
        wide_a,
        far_a,
        wide_stats,
        chip_view,
        chip_a,
        vec,
        *col_pieces,
    )
    loss_value = (loss + swap(loss))[0, 0]
    other_grad = swap(far_grad)
    grad_b = jnp.where(
        c_at == 0,
        jnp.concatenate([near_grad, other_grad], axis=1),
        jnp.concatenate([other_grad, near_grad], axis=1),
    )
    return (grad_a, grad_b, loss_value)


def solution(mesh):
    split = P(("y", "x", "c"), "z")
    chips = Mesh(mesh.devices.reshape(4, 4, 2, 8), ("y", "x", "c", "z"))
    return jax.shard_map(
        local,
        mesh=chips,
        in_specs=(split, split),
        out_specs=(split, split, P()),
        check_vma=False,
    )
```

```python
import functools

import jax
import jax.numpy as jnp
from jax import lax
from jax.experimental import pallas as pl
from jax.experimental.pallas import tpu as pltpu
from jax.sharding import Mesh, PartitionSpec as P

OFF_WEIGHT = 0.0051
EPSILON = 1e-05
F32 = jnp.float32
BF16 = jnp.bfloat16
PLANE = ("y", "x")
CONTRACT_LAST = (((1,), (1,)), ((), ()))
EXTRA = 16
MIB = 1 << 20
VMEM = pl.BlockSpec(memory_space=pltpu.VMEM)
SMEM = pl.BlockSpec(memory_space=pltpu.SMEM)


def shift(value, step, second=False):
    y_size, x_size = lax.axis_size("y"), lax.axis_size("x")
    pairs = []
    for y in range(y_size):
        for x in range(x_size):
            for c in range(2):
                along_y = (c == 1) != second
                to_y = (y + step) % y_size if along_y else y
                to_x = x if along_y else (x + step) % x_size
                pairs.append(((y * x_size + x) * 2 + c, (to_y * x_size + to_x) * 2 + c))
    return lax.ppermute(value, ("y", "x", "c"), pairs)


def swap(value):
    return lax.ppermute(value, "c", [(0, 1), (1, 0)])


def spread(value, axes, size):
    copies = jnp.broadcast_to(value[None], (size,) + value.shape)
    return lax.all_to_all(copies, axes, split_axis=0, concat_axis=0, tiled=True)


def rotate(value, by):
    twice = jnp.concatenate([value, value], axis=0)
    return lax.dynamic_slice_in_dim(twice, by, value.shape[0], axis=0)


def others(value, second=False):
    return [shift(value, step, second) for step in (1, 3, 2)]


def normalise(raw, mean, inverse):
    return ((raw.astype(F32) - mean) * inverse).astype(BF16)


def rounded(raw, mean, inverse):
    return lax.reduce_precision((raw.astype(F32) - mean) * inverse, 8, 7).astype(BF16)


def widen_body(at, stats, raw, keep, give, held, done):
    blocks, _, half = keep.shape
    copies = [
        pltpu.make_async_copy(raw.at[g], held.at[g], done.at[g]) for g in range(blocks)
    ]
    for copy in copies:
        copy.start()
    for g in range(blocks):
        copies[g].wait()
        for place, out in enumerate((keep, give)):
            spot = 1 - at[2] if place else at[2]
            cols = pl.ds(pl.multiple_of(spot * half, half), half)
            out[g] = normalise(held[g, :, cols], stats[g, 1:2, cols], stats[g, 3:4, cols])


def widen(at, stats, raw):
    blocks, rows, width = raw.shape
    return pl.pallas_call(
        widen_body,
        in_specs=[SMEM, VMEM, pl.BlockSpec(memory_space=pltpu.HBM)],
        out_specs=[VMEM] * 2,
        out_shape=[jax.ShapeDtypeStruct((blocks, rows, width // 2), BF16)] * 2,
        scratch_shapes=[pltpu.VMEM(raw.shape, BF16), pltpu.SemaphoreType.DMA((blocks,))],
        compiler_params=pltpu.CompilerParams(vmem_limit_bytes=8 * MIB),
        cost_estimate=pl.CostEstimate(
            flops=6 * blocks * rows * width, bytes_accessed=4 * MIB, transcendentals=0
        ),
        name="widen",
    )(at, stats, raw)


def correlate_body(keep, other, lhs, *parts):
    blocks, rows, half = other.shape
    quarter = lhs.shape[0] // 4
    for g in range(blocks):
        rhs = jnp.concatenate([keep[g], other[g]], axis=0)
        for turned in range(4):
            part = jnp.dot(
                lhs[turned * quarter : (turned + 1) * quarter],
                rhs,
                preferred_element_type=F32,
            )
            parts[turned][g] = part.astype(BF16)


def correlate(keep, other, lhs):
    blocks, rows, half = other.shape
    part = jax.ShapeDtypeStruct((blocks, lhs.shape[0] // 4, half), BF16)
    return pl.pallas_call(
        correlate_body,
        in_specs=[VMEM] * 3,
        out_specs=[VMEM] * 4,
        out_shape=[part] * 4,
        compiler_params=pltpu.CompilerParams(vmem_limit_bytes=6 * MIB),
        cost_estimate=pl.CostEstimate(
            flops=8 * rows * half * half * blocks, bytes_accessed=4 * MIB, transcendentals=0
        ),
        name="correlate",
    )(keep, other, lhs)


def tile_body(scale, at, diagonal, own, ahead, behind, across, pull, outward):
    blocks, quarter, half = pull.shape
    row = lax.broadcasted_iota(jnp.int32, (quarter, half), 0)
    col = lax.broadcasted_iota(jnp.int32, (quarter, half), 1)
    same = col + at[2] * half == row + at[4] * quarter
    size = jnp.zeros((8, half), F32)
    for g in range(blocks):
        total = (own[g].astype(F32) + across[g].astype(F32)) + (
            ahead[g].astype(F32) + behind[g].astype(F32)
        )
        value = jnp.where(same & (at[3] == g), 0.0, scale * total).astype(BF16)
        pull[g] = value
        outward[g, :quarter] = value
        wide = value.astype(F32)
        size = size + jnp.sum((wide * wide).reshape(quarter // 8, 8, half), axis=0)
    share = diagonal[0:1, 0:1] + (0.25 / OFF_WEIGHT) * jnp.sum(size).reshape(1, 1)
    share = jnp.broadcast_to(share, (EXTRA, half))
    high = share.astype(BF16)
    share = share - high.astype(F32)
    middle = share.astype(BF16)
    low = (share - middle.astype(F32)).astype(BF16)
    line = lax.broadcasted_iota(jnp.int32, (EXTRA, half), 0)
    extra = jnp.where(line == 0, high, jnp.where(line == 1, middle, low))
    for g in range(blocks):
        outward[g, quarter:] = extra


def make_tile(at, scale, diagonal, pieces):
    blocks, quarter, half = pieces[0].shape
    return pl.pallas_call(
        functools.partial(tile_body, scale),
        in_specs=[SMEM] + [VMEM] * 5,
        out_specs=[VMEM] * 2,
        out_shape=[
            jax.ShapeDtypeStruct(pieces[0].shape, BF16),
            jax.ShapeDtypeStruct((blocks, quarter + EXTRA, half), BF16),
        ],
        compiler_params=pltpu.CompilerParams(vmem_limit_bytes=6 * MIB),
        cost_estimate=pl.CostEstimate(
            flops=6 * pieces[0].size, bytes_accessed=3 * MIB, transcendentals=0
        ),
        name="tile",
    )(at, diagonal, *pieces)


def place(at, turned, quarter):
    spot = lax.rem(at[4] + turned, 4) * quarter
    return pl.ds(pl.multiple_of(spot, quarter), quarter)


def finish(view, norm, vec, total, extra, weight, mean_row, left_row, images):
    mean, inverse = vec[mean_row : mean_row + 1], vec[mean_row + 2 : mean_row + 3]
    pull, match, left = vec[4:5], vec[5:6], vec[left_row : left_row + 1]
    back = total + norm.astype(F32) * pull
    centre = (extra + pull * left) * (1.0 / images)
    along = weight + pull * match
    white = (view.astype(F32) - mean) * inverse
    return (inverse * (back - centre - white * along)).astype(BF16)


def rows_body(at, near, far, stats, *refs):
    pieces, (near_part, far_part, packed) = refs[:4], refs[4:]
    blocks, rows, half = near.shape
    width = 2 * half
    cols = pl.ds(pl.multiple_of(at[2] * half, half), half)
    ones = jnp.ones((EXTRA, half), BF16)
    size = jnp.zeros((EXTRA, width), F32)
    for g in range(blocks):
        for turned in range(4):
            packed[place(at, turned, width // 4)] = pieces[turned][g]
        rhs = packed[...]
        square = rhs.astype(F32)
        square = (square * square).astype(BF16)
        size = size + lax.dot_general(
            ones, square, CONTRACT_LAST, preferred_element_type=F32
        )
        extra = jnp.broadcast_to(stats[g, 5:6, cols], (EXTRA, half)).astype(BF16)
        lhs = jnp.concatenate([far[g], extra], axis=0)
        far_more = lax.dot_general(lhs, rhs, CONTRACT_LAST, preferred_element_type=F32)
        near_more = lax.dot_general(
            near[g], rhs, CONTRACT_LAST, preferred_element_type=F32
        )
        if g:
            far_part[: rows + EXTRA] += far_more
            near_part[:rows] += near_more
        else:
            far_part[: rows + EXTRA] = far_more
            near_part[:rows] = near_more
    far_part[rows + 8 : rows + EXTRA] = size[:8] * (0.5 / OFF_WEIGHT)
    near_part[rows:] = far_part[rows:]


def cols_body(images, at, near, far, stats, view, norm, vec, *refs):
    pieces, (near_grad, far_grad, loss, packed, total) = refs[:4], refs[4:]
    blocks, rows, width = near.shape
    half = width // 2
    spot = pl.ds(pl.multiple_of(at[2] * half, half), half)
    size = jnp.zeros((1, half), F32)
    for g in range(blocks):
        for turned in range(4):
            packed[g, place(at, turned, width // 4)] = pieces[turned][g, : width // 4]
        rhs = packed[g]
        square = rhs.astype(F32)
        size = size + jnp.sum(square * square, axis=0, keepdims=True)
        extra = jnp.broadcast_to(stats[g, 4:5], (EXTRA, width)).astype(BF16)
        lhs = jnp.concatenate([near[g], far[g], extra], axis=0)
        part = jnp.dot(lhs, rhs, preferred_element_type=F32)
        if g:
            total[...] += part
        else:
            total[...] = part
    shares = []
    for turned in range(4):
        share = jnp.zeros((1, 128), F32)
        for g in range(blocks):
            lines = pieces[turned][g, width // 4 :, :128].astype(F32)
            share = share + ((lines[0:1] + lines[1:2]) + lines[2:3])
        shares.append(share)
    loss[...] = (shares[0] + shares[2]) + (shares[1] + shares[3])
    weight = size * (0.5 / OFF_WEIGHT)
    for which, grad in enumerate((near_grad, far_grad)):
        part = slice(which * rows, (which + 1) * rows)
        grad[...] = finish(
            view[part, spot],
            norm[part, spot],
            vec[:, spot],
            total[part],
            total[2 * rows : 2 * rows + 1],
            weight,
            1,
            6,
            images,
        )


def gradient(body, outs, scratch, name, *operands):
    return pl.pallas_call(
        body,
        in_specs=[SMEM] + [VMEM] * (len(operands) - 1),
        out_specs=[VMEM] * len(outs),
        out_shape=outs,
        scratch_shapes=scratch,
        compiler_params=pltpu.CompilerParams(vmem_limit_bytes=10 * MIB),
        cost_estimate=pl.CostEstimate(
            flops=1 << 30, bytes_accessed=7 * MIB, transcendentals=0
        ),
        name=name,
    )(*operands)


def local(view_a, view_b):
    rows, width = view_a.shape
    chips = lax.axis_size("y") * lax.axis_size("x")
    blocks = lax.axis_size("z")
    images = rows * 2 * chips
    half = width // 2
    x_at, y_at, c_at, z_at = (lax.axis_index(name) for name in ("x", "y", "c", "z"))
    first_at = jnp.where(c_at == 0, x_at, y_at)
    at = jnp.stack([x_at, y_at, c_at, z_at, first_at]).astype(jnp.int32)

    raw_b = lax.all_gather(view_b, "z", axis=0, tiled=False)
    raw_a = lax.all_gather(view_a, "z", axis=0, tiled=False)
    chip_view = jnp.concatenate([view_b, swap(view_b)], axis=0)

    values_a = view_a.astype(F32)
    values_b = view_b.astype(F32)
    local_a = jnp.sum(values_a, axis=0) / rows
    local_b = jnp.sum(values_b, axis=0) / rows
    apart_a = values_a - local_a
    apart_b = values_b - local_b
    mine = jnp.stack(
        [
            local_a,
            local_b,
            jnp.sum(apart_a * apart_a, axis=0),
            jnp.sum(apart_b * apart_b, axis=0),
            jnp.sum(apart_a * apart_b, axis=0),
        ]
    )
    pair = swap(mine)
    gap = mine[:2] - pair[:2]
    joined = jnp.concatenate(
        [
            (mine[:2] + pair[:2]) * 0.5,
            mine[2:4] + pair[2:4] + gap * gap * (rows / 2),
            mine[4:] + pair[4:] + gap[:1] * gap[1:] * (rows / 2),
        ]
    )
    all_stats = spread(joined, PLANE, chips)
    means = jnp.sum(all_stats[:, :2], axis=0) / chips
    away = all_stats[:, :2] - means
    squares = jnp.sum(all_stats[:, 2:4] + 2 * rows * away * away, axis=0)
    cross = jnp.sum(all_stats[:, 4] + 2 * rows * away[:, 0] * away[:, 1], axis=0)
    inverse = lax.rsqrt(squares / images + EPSILON)
    on_diagonal = cross / images * inverse[0] * inverse[1]
    deficit = 1.0 - on_diagonal
    pull_diagonal = lax.reduce_precision(-2.0 * deficit, 8, 7)
    norm_a = rounded(view_a, means[0], inverse[0])
    norm_b = rounded(view_b, means[1], inverse[1])

    left = inverse * (2 * rows * jnp.sum(all_stats[:, :2], axis=0) - images * means)
    stats = jnp.concatenate([means, inverse, left])
    wide_stats = spread(stats, "z", blocks)
    vec = jnp.concatenate([stats[:4], pull_diagonal[None], on_diagonal[None], left])

    chip_a = jnp.concatenate([norm_a, swap(norm_a)], axis=0)
    lhs = rotate(chip_a.T.reshape(4, width // 4, 2 * rows), first_at).reshape(width, 2 * rows)

    diagonal = jnp.sum((deficit * deficit).reshape(4, width // 4), axis=1)
    diagonal = 0.5 * lax.dynamic_slice_in_dim(diagonal, first_at, 1, axis=0)
    diagonal = jnp.broadcast_to(diagonal[None], (1, 128))
    raw_b, wide_stats, lhs, chip_a, chip_view, vec, diagonal = lax.optimization_barrier(
        (raw_b, wide_stats, lhs, chip_a, chip_view, vec, diagonal)
    )
    near_b, give = widen(at, wide_stats, raw_b)
    far_b = swap(give)
    parts = correlate(near_b, far_b, lhs)
    total = parts[0].astype(F32)
    for step in (1, 3, 2):
        total = total + shift(parts[step], step).astype(F32)
    total = total.astype(BF16)
    pull, outward = make_tile(
        at, 2.0 * OFF_WEIGHT / images, diagonal, [total] + others(total, second=True)
    )
    inward = lax.all_to_all(outward, "z", split_axis=0, concat_axis=0, tiled=True)

    ahead, behind, across = others(pull)
    row_pieces = [pull, behind, across, ahead]
    row_pieces, inward, raw_a = lax.optimization_barrier((row_pieces, inward, raw_a))
    ahead, behind, across = others(inward)
    col_pieces = [inward, behind, across, ahead]

    wide_a = rounded(raw_a, wide_stats[:, 0:1], wide_stats[:, 2:3])
    far_a = rounded(swap(raw_a), wide_stats[:, 0:1], wide_stats[:, 2:3])

    part = jax.ShapeDtypeStruct((rows + EXTRA, width), F32)
    near_part, far_part = gradient(
        rows_body,
        [part, part],
        [pltpu.VMEM((width, half), BF16)],
        "rows",
        at,
        near_b,
        far_b,
        wide_stats,
        *row_pieces,
    )
    far_a, far_part = lax.optimization_barrier((far_a, far_part))
    near_part = near_part + swap(far_part)
    grad_a = finish(
        view_a,
        norm_b,
        vec,
        near_part[:rows],
        near_part[rows : rows + 1],
        near_part[rows + 8 : rows + 9],
        0,
        7,
        images,
    )
    near_grad, far_grad, loss = gradient(
        functools.partial(cols_body, images),
        [jax.ShapeDtypeStruct((rows, half), BF16)] * 2 + [jax.ShapeDtypeStruct((1, 128), F32)],
        [pltpu.VMEM((blocks, width, half), BF16), pltpu.VMEM((2 * rows + EXTRA, half), F32)],
        "cols",
        at,
        wide_a,
        far_a,
        wide_stats,
        chip_view,
        chip_a,
        vec,
        *col_pieces,
    )
    loss_value = (loss + swap(loss))[0, 0]
    other_grad = swap(far_grad)
    grad_b = jnp.where(
        c_at == 0,
        jnp.concatenate([near_grad, other_grad], axis=1),
        jnp.concatenate([other_grad, near_grad], axis=1),
    )
    return (grad_a, grad_b, loss_value)


def solution(mesh):
    split = P(("y", "x", "c"), "z")
    chips = Mesh(mesh.devices.reshape(4, 4, 2, 8), ("y", "x", "c", "z"))
    return jax.shard_map(
        local,
        mesh=chips,
        in_specs=(split, split),
        out_specs=(split, split, P()),
        check_vma=False,
    )
```

```python
import functools

import jax
import jax.numpy as jnp
from jax import lax
from jax.experimental import pallas as pl
from jax.experimental.pallas import tpu as pltpu
from jax.sharding import Mesh, PartitionSpec as P

OFF_WEIGHT = 0.0051
EPSILON = 1e-05
F32 = jnp.float32
BF16 = jnp.bfloat16
PLANE = ("y", "x")
CONTRACT_LAST = (((1,), (1,)), ((), ()))
EXTRA = 16
MIB = 1 << 20
VMEM = pl.BlockSpec(memory_space=pltpu.VMEM)
SMEM = pl.BlockSpec(memory_space=pltpu.SMEM)


def shift(value, step, second=False):
    y_size, x_size = lax.axis_size("y"), lax.axis_size("x")
    pairs = []
    for y in range(y_size):
        for x in range(x_size):
            for c in range(2):
                along_y = (c == 1) != second
                to_y = (y + step) % y_size if along_y else y
                to_x = x if along_y else (x + step) % x_size
                pairs.append(((y * x_size + x) * 2 + c, (to_y * x_size + to_x) * 2 + c))
    return lax.ppermute(value, ("y", "x", "c"), pairs)


def swap(value):
    return lax.ppermute(value, "c", [(0, 1), (1, 0)])


def spread(value, axes, size):
    copies = jnp.broadcast_to(value[None], (size,) + value.shape)
    return lax.all_to_all(copies, axes, split_axis=0, concat_axis=0, tiled=True)


def rotate(value, by):
    twice = jnp.concatenate([value, value], axis=0)
    return lax.dynamic_slice_in_dim(twice, by, value.shape[0], axis=0)


def others(value, second=False):
    return [shift(value, step, second) for step in (1, 3, 2)]


def normalise(raw, mean, inverse):
    return ((raw.astype(F32) - mean) * inverse).astype(BF16)


def rounded(raw, mean, inverse):
    return lax.reduce_precision((raw.astype(F32) - mean) * inverse, 8, 7).astype(BF16)


def correlate_body(at, stats, raw, lhs, *parts):
    blocks, _, half = parts[0].shape
    quarter = lhs.shape[0] // 4
    cols = pl.ds(pl.multiple_of(at[2] * half, half), half)
    near_at, far_at = at[2] * blocks, (1 - at[2]) * blocks
    for g in range(blocks):
        mean, inverse = stats[g, 1:2, cols], stats[g, 3:4, cols]
        near = normalise(raw[near_at + g, :, cols], mean, inverse)
        far = normalise(raw[far_at + g, :, cols], mean, inverse)
        rhs = jnp.concatenate([near, far], axis=0)
        for turned in range(4):
            part = jnp.dot(
                lhs[turned * quarter : (turned + 1) * quarter],
                rhs,
                preferred_element_type=F32,
            )
            parts[turned][g] = part.astype(BF16)


def correlate(at, stats, raw, lhs):
    both, rows, width = raw.shape
    blocks, half = both // 2, width // 2
    part = jax.ShapeDtypeStruct((blocks, lhs.shape[0] // 4, half), BF16)
    return pl.pallas_call(
        correlate_body,
        in_specs=[SMEM, VMEM, VMEM, VMEM],
        out_specs=[VMEM] * 4,
        out_shape=[part] * 4,
        compiler_params=pltpu.CompilerParams(vmem_limit_bytes=6 * MIB),
        cost_estimate=pl.CostEstimate(
            flops=8 * rows * half * half * blocks, bytes_accessed=6 * MIB, transcendentals=0
        ),
        name="correlate",
    )(at, stats, raw, lhs)


def tile_body(scale, at, diagonal, own, ahead, behind, across, pull, outward):
    blocks, quarter, half = pull.shape
    row = lax.broadcasted_iota(jnp.int32, (quarter, half), 0)
    col = lax.broadcasted_iota(jnp.int32, (quarter, half), 1)
    same = col + at[2] * half == row + at[4] * quarter
    size = jnp.zeros((8, half), F32)
    for g in range(blocks):
        total = (own[g].astype(F32) + across[g].astype(F32)) + (
            ahead[g].astype(F32) + behind[g].astype(F32)
        )
        value = jnp.where(same & (at[3] == g), 0.0, scale * total).astype(BF16)
        pull[g] = value
        outward[g, :quarter] = value
        wide = value.astype(F32)
        size = size + jnp.sum((wide * wide).reshape(quarter // 8, 8, half), axis=0)
    share = diagonal[0:1, 0:1] + (0.25 / OFF_WEIGHT) * jnp.sum(size).reshape(1, 1)
    share = jnp.broadcast_to(share, (EXTRA, half))
    high = share.astype(BF16)
    share = share - high.astype(F32)
    middle = share.astype(BF16)
    low = (share - middle.astype(F32)).astype(BF16)
    line = lax.broadcasted_iota(jnp.int32, (EXTRA, half), 0)
    extra = jnp.where(line == 0, high, jnp.where(line == 1, middle, low))
    for g in range(blocks):
        outward[g, quarter:] = extra


def make_tile(at, scale, diagonal, pieces):
    blocks, quarter, half = pieces[0].shape
    return pl.pallas_call(
        functools.partial(tile_body, scale),
        in_specs=[SMEM] + [VMEM] * 5,
        out_specs=[VMEM] * 2,
        out_shape=[
            jax.ShapeDtypeStruct(pieces[0].shape, BF16),
            jax.ShapeDtypeStruct((blocks, quarter + EXTRA, half), BF16),
        ],
        compiler_params=pltpu.CompilerParams(vmem_limit_bytes=6 * MIB),
        cost_estimate=pl.CostEstimate(
            flops=6 * pieces[0].size, bytes_accessed=3 * MIB, transcendentals=0
        ),
        name="tile",
    )(at, diagonal, *pieces)


def place(at, turned, quarter):
    spot = lax.rem(at[4] + turned, 4) * quarter
    return pl.ds(pl.multiple_of(spot, quarter), quarter)


def finish(view, norm, vec, total, extra, weight, mean_row, left_row, images):
    mean, inverse = vec[mean_row : mean_row + 1], vec[mean_row + 2 : mean_row + 3]
    pull, match, left = vec[4:5], vec[5:6], vec[left_row : left_row + 1]
    back = total + norm.astype(F32) * pull
    centre = (extra + pull * left) * (1.0 / images)
    along = weight + pull * match
    white = (view.astype(F32) - mean) * inverse
    return (inverse * (back - centre - white * along)).astype(BF16)


def rows_body(at, raw, stats, *refs):
    pieces, (near_part, far_part, packed) = refs[:4], refs[4:]
    both, rows, width = raw.shape
    blocks, half = both // 2, width // 2
    near_at, far_at = at[2] * blocks, (1 - at[2]) * blocks
    cols = pl.ds(pl.multiple_of(at[2] * half, half), half)
    ones = jnp.ones((EXTRA, half), BF16)
    size = jnp.zeros((EXTRA, width), F32)
    for g in range(blocks):
        for turned in range(4):
            packed[place(at, turned, width // 4)] = pieces[turned][g]
        rhs = packed[...]
        square = rhs.astype(F32)
        square = (square * square).astype(BF16)
        size = size + lax.dot_general(
            ones, square, CONTRACT_LAST, preferred_element_type=F32
        )
        extra = jnp.broadcast_to(stats[g, 5:6, cols], (EXTRA, half)).astype(BF16)
        mean, inverse = stats[g, 1:2, cols], stats[g, 3:4, cols]
        near = normalise(raw[near_at + g, :, cols], mean, inverse)
        far = normalise(raw[far_at + g, :, cols], mean, inverse)
        lhs = jnp.concatenate([far, extra], axis=0)
        far_more = lax.dot_general(lhs, rhs, CONTRACT_LAST, preferred_element_type=F32)
        near_more = lax.dot_general(
            near, rhs, CONTRACT_LAST, preferred_element_type=F32
        )
        if g:
            far_part[: rows + EXTRA] += far_more
            near_part[:rows] += near_more
        else:
            far_part[: rows + EXTRA] = far_more
            near_part[:rows] = near_more
    far_part[rows + 8 : rows + EXTRA] = size[:8] * (0.5 / OFF_WEIGHT)
    near_part[rows:] = far_part[rows:]


def cols_body(images, at, near, far, stats, view, norm, vec, *refs):
    pieces, (near_grad, far_grad, loss, packed, total) = refs[:4], refs[4:]
    blocks, rows, width = near.shape
    half = width // 2
    spot = pl.ds(pl.multiple_of(at[2] * half, half), half)
    size = jnp.zeros((1, half), F32)
    for g in range(blocks):
        for turned in range(4):
            packed[g, place(at, turned, width // 4)] = pieces[turned][g, : width // 4]
        rhs = packed[g]
        square = rhs.astype(F32)
        size = size + jnp.sum(square * square, axis=0, keepdims=True)
        extra = jnp.broadcast_to(stats[g, 4:5], (EXTRA, width)).astype(BF16)
        lhs = jnp.concatenate([near[g], far[g], extra], axis=0)
        part = jnp.dot(lhs, rhs, preferred_element_type=F32)
        if g:
            total[...] += part
        else:
            total[...] = part
    shares = []
    for turned in range(4):
        share = jnp.zeros((1, 128), F32)
        for g in range(blocks):
            lines = pieces[turned][g, width // 4 :, :128].astype(F32)
            share = share + ((lines[0:1] + lines[1:2]) + lines[2:3])
        shares.append(share)
    loss[...] = (shares[0] + shares[2]) + (shares[1] + shares[3])
    weight = size * (0.5 / OFF_WEIGHT)
    for which, grad in enumerate((near_grad, far_grad)):
        part = slice(which * rows, (which + 1) * rows)
        grad[...] = finish(
            view[part, spot],
            norm[part, spot],
            vec[:, spot],
            total[part],
            total[2 * rows : 2 * rows + 1],
            weight,
            1,
            6,
            images,
        )


def gradient(body, outs, scratch, name, *operands):
    return pl.pallas_call(
        body,
        in_specs=[SMEM] + [VMEM] * (len(operands) - 1),
        out_specs=[VMEM] * len(outs),
        out_shape=outs,
        scratch_shapes=scratch,
        compiler_params=pltpu.CompilerParams(vmem_limit_bytes=10 * MIB),
        cost_estimate=pl.CostEstimate(
            flops=1 << 30, bytes_accessed=7 * MIB, transcendentals=0
        ),
        name=name,
    )(*operands)


def local(view_a, view_b):
    rows, width = view_a.shape
    chips = lax.axis_size("y") * lax.axis_size("x")
    blocks = lax.axis_size("z")
    images = rows * 2 * chips
    half = width // 2
    x_at, y_at, c_at, z_at = (lax.axis_index(name) for name in ("x", "y", "c", "z"))
    first_at = jnp.where(c_at == 0, x_at, y_at)
    at = jnp.stack([x_at, y_at, c_at, z_at, first_at]).astype(jnp.int32)

    raw_b = lax.all_gather(view_b, ("c", "z"), axis=0, tiled=False)
    raw_a = lax.all_gather(view_a, "z", axis=0, tiled=False)
    chip_view = jnp.concatenate([view_b, swap(view_b)], axis=0)

    values_a = view_a.astype(F32)
    values_b = view_b.astype(F32)
    local_a = jnp.sum(values_a, axis=0) / rows
    local_b = jnp.sum(values_b, axis=0) / rows
    apart_a = values_a - local_a
    apart_b = values_b - local_b
    mine = jnp.stack(
        [
            local_a,
            local_b,
            jnp.sum(apart_a * apart_a, axis=0),
            jnp.sum(apart_b * apart_b, axis=0),
            jnp.sum(apart_a * apart_b, axis=0),
        ]
    )
    pair = swap(mine)
    gap = mine[:2] - pair[:2]
    joined = jnp.concatenate(
        [
            (mine[:2] + pair[:2]) * 0.5,
            mine[2:4] + pair[2:4] + gap * gap * (rows / 2),
            mine[4:] + pair[4:] + gap[:1] * gap[1:] * (rows / 2),
        ]
    )
    all_stats = spread(joined, PLANE, chips)
    means = jnp.sum(all_stats[:, :2], axis=0) / chips
    away = all_stats[:, :2] - means
    squares = jnp.sum(all_stats[:, 2:4] + 2 * rows * away * away, axis=0)
    cross = jnp.sum(all_stats[:, 4] + 2 * rows * away[:, 0] * away[:, 1], axis=0)
    inverse = lax.rsqrt(squares / images + EPSILON)
    on_diagonal = cross / images * inverse[0] * inverse[1]
    deficit = 1.0 - on_diagonal
    pull_diagonal = lax.reduce_precision(-2.0 * deficit, 8, 7)
    norm_a = rounded(view_a, means[0], inverse[0])
    norm_b = rounded(view_b, means[1], inverse[1])

    left = inverse * (2 * rows * jnp.sum(all_stats[:, :2], axis=0) - images * means)
    stats = jnp.concatenate([means, inverse, left])
    wide_stats = spread(stats, "z", blocks)
    vec = jnp.concatenate([stats[:4], pull_diagonal[None], on_diagonal[None], left])

    chip_a = jnp.concatenate([norm_a, swap(norm_a)], axis=0)
    lhs = rotate(chip_a.T.reshape(4, width // 4, 2 * rows), first_at).reshape(width, 2 * rows)

    diagonal = jnp.sum((deficit * deficit).reshape(4, width // 4), axis=1)
    diagonal = 0.5 * lax.dynamic_slice_in_dim(diagonal, first_at, 1, axis=0)
    diagonal = jnp.broadcast_to(diagonal[None], (1, 128))
    raw_b, wide_stats, lhs, chip_a, chip_view, vec, diagonal = lax.optimization_barrier(
        (raw_b, wide_stats, lhs, chip_a, chip_view, vec, diagonal)
    )
    parts = correlate(at, wide_stats, raw_b, lhs)
    total = parts[0].astype(F32)
    for step in (1, 3, 2):
        total = total + shift(parts[step], step).astype(F32)
    total = total.astype(BF16)
    pull, outward = make_tile(
        at, 2.0 * OFF_WEIGHT / images, diagonal, [total] + others(total, second=True)
    )
    inward = lax.all_to_all(outward, "z", split_axis=0, concat_axis=0, tiled=True)

    ahead, behind, across = others(pull)
    row_pieces = [pull, behind, across, ahead]
    row_pieces, inward, raw_a = lax.optimization_barrier((row_pieces, inward, raw_a))
    ahead, behind, across = others(inward)
    col_pieces = [inward, behind, across, ahead]

    wide_a = rounded(raw_a, wide_stats[:, 0:1], wide_stats[:, 2:3])
    far_a = rounded(swap(raw_a), wide_stats[:, 0:1], wide_stats[:, 2:3])

    part = jax.ShapeDtypeStruct((rows + EXTRA, width), F32)
    near_part, far_part = gradient(
        rows_body,
        [part, part],
        [pltpu.VMEM((width, half), BF16)],
        "rows",
        at,
        raw_b,
        wide_stats,
        *row_pieces,
    )
    far_a, far_part = lax.optimization_barrier((far_a, far_part))
    near_part = near_part + swap(far_part)
    grad_a = finish(
        view_a,
        norm_b,
        vec,
        near_part[:rows],
        near_part[rows : rows + 1],
        near_part[rows + 8 : rows + 9],
        0,
        7,
        images,
    )
    near_grad, far_grad, loss = gradient(
        functools.partial(cols_body, images),
        [jax.ShapeDtypeStruct((rows, half), BF16)] * 2 + [jax.ShapeDtypeStruct((1, 128), F32)],
        [pltpu.VMEM((blocks, width, half), BF16), pltpu.VMEM((2 * rows + EXTRA, half), F32)],
        "cols",
        at,
        wide_a,
        far_a,
        wide_stats,
        chip_view,
        chip_a,
        vec,
        *col_pieces,
    )
    loss_value = (loss + swap(loss))[0, 0]
    other_grad = swap(far_grad)
    grad_b = jnp.where(
        c_at == 0,
        jnp.concatenate([near_grad, other_grad], axis=1),
        jnp.concatenate([other_grad, near_grad], axis=1),
    )
    return (grad_a, grad_b, loss_value)


def solution(mesh):
    split = P(("y", "x", "c"), "z")
    chips = Mesh(mesh.devices.reshape(4, 4, 2, 8), ("y", "x", "c", "z"))
    return jax.shard_map(
        local,
        mesh=chips,
        in_specs=(split, split),
        out_specs=(split, split, P()),
        check_vma=False,
    )
```

```python
import functools

import jax
import jax.numpy as jnp
from jax import lax
from jax.experimental import pallas as pl
from jax.experimental.pallas import tpu as pltpu
from jax.sharding import Mesh, PartitionSpec as P

OFF_WEIGHT = 0.0051
EPSILON = 1e-05
F32 = jnp.float32
BF16 = jnp.bfloat16
PLANE = ("y", "x")
CONTRACT_LAST = (((1,), (1,)), ((), ()))
EXTRA = 16
MIB = 1 << 20
VMEM = pl.BlockSpec(memory_space=pltpu.VMEM)
SMEM = pl.BlockSpec(memory_space=pltpu.SMEM)


def shift(value, step, second=False):
    y_size, x_size = lax.axis_size("y"), lax.axis_size("x")
    pairs = []
    for y in range(y_size):
        for x in range(x_size):
            for c in range(2):
                along_y = (c == 1) != second
                to_y = (y + step) % y_size if along_y else y
                to_x = x if along_y else (x + step) % x_size
                pairs.append(((y * x_size + x) * 2 + c, (to_y * x_size + to_x) * 2 + c))
    return lax.ppermute(value, ("y", "x", "c"), pairs)


def swap(value):
    return lax.ppermute(value, "c", [(0, 1), (1, 0)])


def spread(value, axes, size):
    copies = jnp.broadcast_to(value[None], (size,) + value.shape)
    return lax.all_to_all(copies, axes, split_axis=0, concat_axis=0, tiled=True)


def rotate(value, by):
    twice = jnp.concatenate([value, value], axis=0)
    return lax.dynamic_slice_in_dim(twice, by, value.shape[0], axis=0)


def others(value, second=False):
    return [shift(value, step, second) for step in (1, 3, 2)]


def normalise(raw, mean, inverse):
    return ((raw.astype(F32) - mean) * inverse).astype(BF16)


def rounded(raw, mean, inverse):
    return lax.reduce_precision((raw.astype(F32) - mean) * inverse, 8, 7).astype(BF16)


def correlate_body(at, stats, raw, lhs, *parts):
    blocks, _, half = parts[0].shape
    quarter = lhs.shape[0] // 4
    cols = pl.ds(pl.multiple_of(at[2] * half, half), half)
    near_at, far_at = at[2] * blocks, (1 - at[2]) * blocks
    for g in range(blocks):
        mean, inverse = stats[g, 1:2, cols], stats[g, 3:4, cols]
        near = normalise(raw[near_at + g, :, cols], mean, inverse)
        far = normalise(raw[far_at + g, :, cols], mean, inverse)
        rhs = jnp.concatenate([near, far], axis=0)
        for turned in range(4):
            part = jnp.dot(
                lhs[turned * quarter : (turned + 1) * quarter],
                rhs,
                preferred_element_type=F32,
            )
            parts[turned][g] = part.astype(BF16)


def correlate(at, stats, raw, lhs):
    both, rows, width = raw.shape
    blocks, half = both // 2, width // 2
    part = jax.ShapeDtypeStruct((blocks, lhs.shape[0] // 4, half), BF16)
    return pl.pallas_call(
        correlate_body,
        in_specs=[SMEM, VMEM, VMEM, VMEM],
        out_specs=[VMEM] * 4,
        out_shape=[part] * 4,
        compiler_params=pltpu.CompilerParams(vmem_limit_bytes=6 * MIB),
        cost_estimate=pl.CostEstimate(
            flops=8 * rows * half * half * blocks, bytes_accessed=6 * MIB, transcendentals=0
        ),
        name="correlate",
    )(at, stats, raw, lhs)


def tile_body(scale, at, diagonal, own, ahead, behind, across, pull, outward):
    blocks, quarter, half = pull.shape
    row = lax.broadcasted_iota(jnp.int32, (quarter, half), 0)
    col = lax.broadcasted_iota(jnp.int32, (quarter, half), 1)
    same = col + at[2] * half == row + at[4] * quarter
    size = jnp.zeros((8, half), F32)
    for g in range(blocks):
        total = (own[g].astype(F32) + across[g].astype(F32)) + (
            ahead[g].astype(F32) + behind[g].astype(F32)
        )
        value = jnp.where(same & (at[3] == g), 0.0, scale * total).astype(BF16)
        pull[g] = value
        outward[g, :quarter] = value
        wide = value.astype(F32)
        size = size + jnp.sum((wide * wide).reshape(quarter // 8, 8, half), axis=0)
    share = diagonal[0:1, 0:1] + (0.25 / OFF_WEIGHT) * jnp.sum(size).reshape(1, 1)
    share = jnp.broadcast_to(share, (EXTRA, half))
    high = share.astype(BF16)
    share = share - high.astype(F32)
    middle = share.astype(BF16)
    low = (share - middle.astype(F32)).astype(BF16)
    line = lax.broadcasted_iota(jnp.int32, (EXTRA, half), 0)
    extra = jnp.where(line == 0, high, jnp.where(line == 1, middle, low))
    for g in range(blocks):
        outward[g, quarter:] = extra


def make_tile(at, scale, diagonal, pieces):
    blocks, quarter, half = pieces[0].shape
    return pl.pallas_call(
        functools.partial(tile_body, scale),
        in_specs=[SMEM] + [VMEM] * 5,
        out_specs=[VMEM] * 2,
        out_shape=[
            jax.ShapeDtypeStruct(pieces[0].shape, BF16),
            jax.ShapeDtypeStruct((blocks, quarter + EXTRA, half), BF16),
        ],
        compiler_params=pltpu.CompilerParams(vmem_limit_bytes=6 * MIB),
        cost_estimate=pl.CostEstimate(
            flops=6 * pieces[0].size, bytes_accessed=3 * MIB, transcendentals=0
        ),
        name="tile",
    )(at, diagonal, *pieces)


def place(at, turned, quarter):
    spot = lax.rem(at[4] + turned, 4) * quarter
    return pl.ds(pl.multiple_of(spot, quarter), quarter)


def finish(view, norm, vec, total, extra, weight, mean_row, left_row, images):
    mean, inverse = vec[mean_row : mean_row + 1], vec[mean_row + 2 : mean_row + 3]
    pull, match, left = vec[4:5], vec[5:6], vec[left_row : left_row + 1]
    back = total + norm.astype(F32) * pull
    centre = (extra + pull * left) * (1.0 / images)
    along = weight + pull * match
    white = (view.astype(F32) - mean) * inverse
    return (inverse * (back - centre - white * along)).astype(BF16)


def rows_body(at, raw, stats, *refs):
    pieces, (near_part, far_part, packed) = refs[:4], refs[4:]
    both, rows, width = raw.shape
    blocks, half = both // 2, width // 2
    near_at, far_at = at[2] * blocks, (1 - at[2]) * blocks
    cols = pl.ds(pl.multiple_of(at[2] * half, half), half)
    ones = jnp.ones((EXTRA, half), BF16)
    size = jnp.zeros((EXTRA, width), F32)
    for g in range(blocks):
        for turned in range(4):
            packed[place(at, turned, width // 4)] = pieces[turned][g]
        rhs = packed[...]
        square = rhs.astype(F32)
        square = (square * square).astype(BF16)
        size = size + lax.dot_general(
            ones, square, CONTRACT_LAST, preferred_element_type=F32
        )
        extra = jnp.broadcast_to(stats[g, 5:6, cols], (EXTRA, half)).astype(BF16)
        mean, inverse = stats[g, 1:2, cols], stats[g, 3:4, cols]
        near = normalise(raw[near_at + g, :, cols], mean, inverse)
        far = normalise(raw[far_at + g, :, cols], mean, inverse)
        lhs = jnp.concatenate([far, extra], axis=0)
        far_more = lax.dot_general(lhs, rhs, CONTRACT_LAST, preferred_element_type=F32)
        near_more = lax.dot_general(
            near, rhs, CONTRACT_LAST, preferred_element_type=F32
        )
        if g:
            far_part[: rows + EXTRA] += far_more
            near_part[:rows] += near_more
        else:
            far_part[: rows + EXTRA] = far_more
            near_part[:rows] = near_more
    far_part[rows + 8 : rows + EXTRA] = size[:8] * (0.5 / OFF_WEIGHT)
    near_part[rows:] = far_part[rows:]


def cols_body(images, at, near, far, stats, view, norm, vec, *refs):
    pieces, (near_grad, far_grad, loss, packed, total) = refs[:4], refs[4:]
    blocks, rows, width = near.shape
    half = width // 2
    spot = pl.ds(pl.multiple_of(at[2] * half, half), half)
    size = jnp.zeros((1, half), F32)
    for g in range(blocks):
        for turned in range(4):
            packed[g, place(at, turned, width // 4)] = pieces[turned][g, : width // 4]
        rhs = packed[g]
        square = rhs.astype(F32)
        size = size + jnp.sum(square * square, axis=0, keepdims=True)
        extra = jnp.broadcast_to(stats[g, 4:5], (EXTRA, width)).astype(BF16)
        lhs = jnp.concatenate([near[g], far[g], extra], axis=0)
        part = jnp.dot(lhs, rhs, preferred_element_type=F32)
        if g:
            total[...] += part
        else:
            total[...] = part
    shares = []
    for turned in range(4):
        share = jnp.zeros((1, 128), F32)
        for g in range(blocks):
            lines = pieces[turned][g, width // 4 :, :128].astype(F32)
            share = share + ((lines[0:1] + lines[1:2]) + lines[2:3])
        shares.append(share)
    loss[...] = (shares[0] + shares[2]) + (shares[1] + shares[3])
    weight = size * (0.5 / OFF_WEIGHT)
    for which, grad in enumerate((near_grad, far_grad)):
        part = slice(which * rows, (which + 1) * rows)
        grad[...] = finish(
            view[part, spot],
            norm[part, spot],
            vec[:, spot],
            total[part],
            total[2 * rows : 2 * rows + 1],
            weight,
            1,
            6,
            images,
        )


def gradient(body, outs, scratch, name, *operands):
    return pl.pallas_call(
        body,
        in_specs=[SMEM] + [VMEM] * (len(operands) - 1),
        out_specs=[VMEM] * len(outs),
        out_shape=outs,
        scratch_shapes=scratch,
        compiler_params=pltpu.CompilerParams(vmem_limit_bytes=10 * MIB),
        cost_estimate=pl.CostEstimate(
            flops=1 << 30, bytes_accessed=7 * MIB, transcendentals=0
        ),
        name=name,
    )(*operands)


def join_body(
    images, at, near, other, loss, other_loss, near_part, far_part, view, norm, vec, grad_a, grad_b, total
):
    rows, half = near.shape
    for which, value in enumerate((near, other)):
        spot = (1 - at[2] if which else at[2]) * half
        grad_b[:, pl.ds(pl.multiple_of(spot, half), half)] = value[...]
    total[...] = loss[...] + other_loss[...]
    ends = near_part[rows:] + far_part[rows:]
    for line in range(0, rows, 64):
        lines = slice(line, line + 64)
        grad_a[lines] = finish(
            view[lines],
            norm[lines],
            vec,
            near_part[lines] + far_part[lines],
            ends[0:1],
            ends[8:9],
            0,
            7,
            images,
        )


def join(images, at, near, *operands):
    rows, half = near.shape
    grad = jax.ShapeDtypeStruct((rows, 2 * half), BF16)
    return pl.pallas_call(
        functools.partial(join_body, images),
        in_specs=[SMEM] + [VMEM] * (1 + len(operands)),
        out_specs=[VMEM] * 3,
        out_shape=[grad, grad, jax.ShapeDtypeStruct((1, 128), F32)],
        compiler_params=pltpu.CompilerParams(vmem_limit_bytes=6 * MIB),
        cost_estimate=pl.CostEstimate(flops=MIB, bytes_accessed=2 * MIB, transcendentals=0),
        name="join",
    )(at, near, *operands)


def local(view_a, view_b):
    rows, width = view_a.shape
    chips = lax.axis_size("y") * lax.axis_size("x")
    blocks = lax.axis_size("z")
    images = rows * 2 * chips
    half = width // 2
    x_at, y_at, c_at, z_at = (lax.axis_index(name) for name in ("x", "y", "c", "z"))
    first_at = jnp.where(c_at == 0, x_at, y_at)
    at = jnp.stack([x_at, y_at, c_at, z_at, first_at]).astype(jnp.int32)

    raw_b = lax.all_gather(view_b, ("c", "z"), axis=0, tiled=False)
    raw_a = lax.all_gather(view_a, "z", axis=0, tiled=False)
    chip_view = jnp.concatenate([view_b, swap(view_b)], axis=0)

    values_a = view_a.astype(F32)
    values_b = view_b.astype(F32)
    local_a = jnp.sum(values_a, axis=0) / rows
    local_b = jnp.sum(values_b, axis=0) / rows
    apart_a = values_a - local_a
    apart_b = values_b - local_b
    mine = jnp.stack(
        [
            local_a,
            local_b,
            jnp.sum(apart_a * apart_a, axis=0),
            jnp.sum(apart_b * apart_b, axis=0),
            jnp.sum(apart_a * apart_b, axis=0),
        ]
    )
    pair = swap(mine)
    gap = mine[:2] - pair[:2]
    joined = jnp.concatenate(
        [
            (mine[:2] + pair[:2]) * 0.5,
            mine[2:4] + pair[2:4] + gap * gap * (rows / 2),
            mine[4:] + pair[4:] + gap[:1] * gap[1:] * (rows / 2),
        ]
    )
    all_stats = spread(joined, PLANE, chips)
    means = jnp.sum(all_stats[:, :2], axis=0) / chips
    away = all_stats[:, :2] - means
    squares = jnp.sum(all_stats[:, 2:4] + 2 * rows * away * away, axis=0)
    cross = jnp.sum(all_stats[:, 4] + 2 * rows * away[:, 0] * away[:, 1], axis=0)
    inverse = lax.rsqrt(squares / images + EPSILON)
    on_diagonal = cross / images * inverse[0] * inverse[1]
    deficit = 1.0 - on_diagonal
    pull_diagonal = lax.reduce_precision(-2.0 * deficit, 8, 7)
    norm_a = rounded(view_a, means[0], inverse[0])
    norm_b = rounded(view_b, means[1], inverse[1])

    left = inverse * (2 * rows * jnp.sum(all_stats[:, :2], axis=0) - images * means)
    stats = jnp.concatenate([means, inverse, left])
    wide_stats = spread(stats, "z", blocks)
    vec = jnp.concatenate([stats[:4], pull_diagonal[None], on_diagonal[None], left])

    chip_a = jnp.concatenate([norm_a, swap(norm_a)], axis=0)
    lhs = rotate(chip_a.T.reshape(4, width // 4, 2 * rows), first_at).reshape(width, 2 * rows)

    diagonal = jnp.sum((deficit * deficit).reshape(4, width // 4), axis=1)
    diagonal = 0.5 * lax.dynamic_slice_in_dim(diagonal, first_at, 1, axis=0)
    diagonal = jnp.broadcast_to(diagonal[None], (1, 128))
    raw_b, wide_stats, lhs, chip_a, chip_view, vec, diagonal = lax.optimization_barrier(
        (raw_b, wide_stats, lhs, chip_a, chip_view, vec, diagonal)
    )
    parts = correlate(at, wide_stats, raw_b, lhs)
    total = parts[0].astype(F32)
    for step in (1, 3, 2):
        total = total + shift(parts[step], step).astype(F32)
    total = total.astype(BF16)
    pull, outward = make_tile(
        at, 2.0 * OFF_WEIGHT / images, diagonal, [total] + others(total, second=True)
    )
    inward = lax.all_to_all(outward, "z", split_axis=0, concat_axis=0, tiled=True)

    ahead, behind, across = others(pull)
    row_pieces = [pull, behind, across, ahead]
    row_pieces, inward, raw_a = lax.optimization_barrier((row_pieces, inward, raw_a))
    ahead, behind, across = others(inward)
    col_pieces = [inward, behind, across, ahead]

    wide_a = rounded(raw_a, wide_stats[:, 0:1], wide_stats[:, 2:3])
    far_a = rounded(swap(raw_a), wide_stats[:, 0:1], wide_stats[:, 2:3])

    part = jax.ShapeDtypeStruct((rows + EXTRA, width), F32)
    near_part, far_part = gradient(
        rows_body,
        [part, part],
        [pltpu.VMEM((width, half), BF16)],
        "rows",
        at,
        raw_b,
        wide_stats,
        *row_pieces,
    )
    far_a, far_part = lax.optimization_barrier((far_a, far_part))
    near_grad, far_grad, loss = gradient(
        functools.partial(cols_body, images),
        [jax.ShapeDtypeStruct((rows, half), BF16)] * 2 + [jax.ShapeDtypeStruct((1, 128), F32)],
        [pltpu.VMEM((blocks, width, half), BF16), pltpu.VMEM((2 * rows + EXTRA, half), F32)],
        "cols",
        at,
        wide_a,
        far_a,
        wide_stats,
        chip_view,
        chip_a,
        vec,
        *col_pieces,
    )
    grad_a, grad_b, total_loss = join(
        images,
        at,
        near_grad,
        swap(far_grad),
        loss,
        swap(loss),
        near_part,
        swap(far_part),
        view_a,
        norm_b,
        vec,
    )
    loss_value = total_loss[0, 0]
    return (grad_a, grad_b, loss_value)


def solution(mesh):
    split = P(("y", "x", "c"), "z")
    chips = Mesh(mesh.devices.reshape(4, 4, 2, 8), ("y", "x", "c", "z"))
    return jax.shard_map(
        local,
        mesh=chips,
        in_specs=(split, split),
        out_specs=(split, split, P()),
        check_vma=False,
    )
```

```python
import functools

import jax
import jax.numpy as jnp
from jax import lax
from jax.experimental import pallas as pl
from jax.experimental.pallas import tpu as pltpu
from jax.sharding import Mesh, PartitionSpec as P

OFF_WEIGHT = 0.0051
EPSILON = 1e-05
F32 = jnp.float32
BF16 = jnp.bfloat16
PLANE = ("y", "x")
CONTRACT_LAST = (((1,), (1,)), ((), ()))
EXTRA = 16
MIB = 1 << 20
VMEM = pl.BlockSpec(memory_space=pltpu.VMEM)
SMEM = pl.BlockSpec(memory_space=pltpu.SMEM)


def shift(value, step, second=False):
    y_size, x_size = lax.axis_size("y"), lax.axis_size("x")
    pairs = []
    for y in range(y_size):
        for x in range(x_size):
            for c in range(2):
                along_y = (c == 1) != second
                to_y = (y + step) % y_size if along_y else y
                to_x = x if along_y else (x + step) % x_size
                pairs.append(((y * x_size + x) * 2 + c, (to_y * x_size + to_x) * 2 + c))
    return lax.ppermute(value, ("y", "x", "c"), pairs)


def swap(value):
    return lax.ppermute(value, "c", [(0, 1), (1, 0)])


def spread(value, axes, size):
    copies = jnp.broadcast_to(value[None], (size,) + value.shape)
    return lax.all_to_all(copies, axes, split_axis=0, concat_axis=0, tiled=True)


def rotate(value, by):
    twice = jnp.concatenate([value, value], axis=0)
    return lax.dynamic_slice_in_dim(twice, by, value.shape[0], axis=0)


def others(value, second=False):
    return [shift(value, step, second) for step in (1, 3, 2)]


def normalise(raw, mean, inverse):
    return ((raw.astype(F32) - mean) * inverse).astype(BF16)


def rounded(raw, mean, inverse):
    return lax.reduce_precision((raw.astype(F32) - mean) * inverse, 8, 7).astype(BF16)


def correlate_body(at, stats, raw, lhs, *parts):
    blocks, _, half = parts[0].shape
    quarter = lhs.shape[0] // 4
    cols = pl.ds(pl.multiple_of(at[2] * half, half), half)
    near_at, far_at = at[2] * blocks, (1 - at[2]) * blocks
    for g in range(blocks):
        mean, inverse = stats[g, 1:2, cols], stats[g, 3:4, cols]
        near = normalise(raw[near_at + g, :, cols], mean, inverse)
        far = normalise(raw[far_at + g, :, cols], mean, inverse)
        rhs = jnp.concatenate([near, far], axis=0)
        for turned in range(4):
            part = jnp.dot(
                lhs[turned * quarter : (turned + 1) * quarter],
                rhs,
                preferred_element_type=F32,
            )
            parts[turned][g] = part.astype(BF16)


def correlate(at, stats, raw, lhs):
    both, rows, width = raw.shape
    blocks, half = both // 2, width // 2
    part = jax.ShapeDtypeStruct((blocks, lhs.shape[0] // 4, half), BF16)
    return pl.pallas_call(
        correlate_body,
        in_specs=[SMEM, VMEM, VMEM, VMEM],
        out_specs=[VMEM] * 4,
        out_shape=[part] * 4,
        compiler_params=pltpu.CompilerParams(vmem_limit_bytes=6 * MIB),
        cost_estimate=pl.CostEstimate(
            flops=8 * rows * half * half * blocks, bytes_accessed=6 * MIB, transcendentals=0
        ),
        name="correlate",
    )(at, stats, raw, lhs)


def tile_body(scale, at, diagonal, own, ahead, behind, across, pull, outward):
    blocks, quarter, half = pull.shape
    row = lax.broadcasted_iota(jnp.int32, (quarter, half), 0)
    col = lax.broadcasted_iota(jnp.int32, (quarter, half), 1)
    same = col + at[2] * half == row + at[4] * quarter
    size = jnp.zeros((8, half), F32)
    for g in range(blocks):
        total = (own[g].astype(F32) + across[g].astype(F32)) + (
            ahead[g].astype(F32) + behind[g].astype(F32)
        )
        value = jnp.where(same & (at[3] == g), 0.0, scale * total).astype(BF16)
        pull[g] = value
        outward[g, :quarter] = value
        wide = value.astype(F32)
        size = size + jnp.sum((wide * wide).reshape(quarter // 8, 8, half), axis=0)
    share = diagonal[0:1, 0:1] + (0.25 / OFF_WEIGHT) * jnp.sum(size).reshape(1, 1)
    share = jnp.broadcast_to(share, (EXTRA, half))
    high = share.astype(BF16)
    share = share - high.astype(F32)
    middle = share.astype(BF16)
    low = (share - middle.astype(F32)).astype(BF16)
    line = lax.broadcasted_iota(jnp.int32, (EXTRA, half), 0)
    extra = jnp.where(line == 0, high, jnp.where(line == 1, middle, low))
    for g in range(blocks):
        outward[g, quarter:] = extra


def make_tile(at, scale, diagonal, pieces):
    blocks, quarter, half = pieces[0].shape
    return pl.pallas_call(
        functools.partial(tile_body, scale),
        in_specs=[SMEM] + [VMEM] * 5,
        out_specs=[VMEM] * 2,
        out_shape=[
            jax.ShapeDtypeStruct(pieces[0].shape, BF16),
            jax.ShapeDtypeStruct((blocks, quarter + EXTRA, half), BF16),
        ],
        compiler_params=pltpu.CompilerParams(vmem_limit_bytes=6 * MIB),
        cost_estimate=pl.CostEstimate(
            flops=6 * pieces[0].size, bytes_accessed=3 * MIB, transcendentals=0
        ),
        name="tile",
    )(at, diagonal, *pieces)


def place(at, turned, quarter):
    spot = lax.rem(at[4] + turned, 4) * quarter
    return pl.ds(pl.multiple_of(spot, quarter), quarter)


def finish(view, norm, vec, total, extra, weight, mean_row, left_row, images):
    mean, inverse = vec[mean_row : mean_row + 1], vec[mean_row + 2 : mean_row + 3]
    pull, match, left = vec[4:5], vec[5:6], vec[left_row : left_row + 1]
    back = total + norm.astype(F32) * pull
    centre = (extra + pull * left) * (1.0 / images)
    along = weight + pull * match
    white = (view.astype(F32) - mean) * inverse
    return (inverse * (back - centre - white * along)).astype(BF16)


def gather_share(lines):
    lines = lines.astype(F32)
    return (lines[0:1] + lines[1:2]) + lines[2:3]


def compact_body(inward, out):
    blocks, lines, half = inward.shape
    quarter = lines - EXTRA
    share = jnp.zeros((1, half), F32)
    for g in range(blocks):
        out[g * quarter : (g + 1) * quarter] = inward[g, :quarter]
        share = share + gather_share(inward[g, quarter:])
    share = jnp.broadcast_to(share, (EXTRA, half))
    high = share.astype(BF16)
    share = share - high.astype(F32)
    middle = share.astype(BF16)
    low = (share - middle.astype(F32)).astype(BF16)
    line = lax.broadcasted_iota(jnp.int32, (EXTRA, half), 0)
    out[blocks * quarter :] = jnp.where(line == 0, high, jnp.where(line == 1, middle, low))


def compact(inward):
    blocks, lines, half = inward.shape
    return pl.pallas_call(
        compact_body,
        in_specs=[VMEM],
        out_specs=VMEM,
        out_shape=jax.ShapeDtypeStruct((blocks * (lines - EXTRA) + EXTRA, half), BF16),
        compiler_params=pltpu.CompilerParams(vmem_limit_bytes=2 * MIB),
        cost_estimate=pl.CostEstimate(flops=1, bytes_accessed=MIB, transcendentals=0),
        name="compact",
    )(inward)


def rows_body(at, raw, stats, *refs):
    pieces, (near_part, far_part, packed) = refs[:4], refs[4:]
    both, rows, width = raw.shape
    blocks, half = both // 2, width // 2
    near_at, far_at = at[2] * blocks, (1 - at[2]) * blocks
    cols = pl.ds(pl.multiple_of(at[2] * half, half), half)
    ones = jnp.ones((EXTRA, half), BF16)
    size = jnp.zeros((EXTRA, width), F32)
    for g in range(blocks):
        for turned in range(4):
            packed[place(at, turned, width // 4)] = pieces[turned][g]
        rhs = packed[...]
        square = rhs.astype(F32)
        square = (square * square).astype(BF16)
        size = size + lax.dot_general(
            ones, square, CONTRACT_LAST, preferred_element_type=F32
        )
        extra = jnp.broadcast_to(stats[g, 5:6, cols], (EXTRA, half)).astype(BF16)
        mean, inverse = stats[g, 1:2, cols], stats[g, 3:4, cols]
        near = normalise(raw[near_at + g, :, cols], mean, inverse)
        far = normalise(raw[far_at + g, :, cols], mean, inverse)
        lhs = jnp.concatenate([far, extra], axis=0)
        far_more = lax.dot_general(lhs, rhs, CONTRACT_LAST, preferred_element_type=F32)
        near_more = lax.dot_general(
            near, rhs, CONTRACT_LAST, preferred_element_type=F32
        )
        if g:
            far_part[: rows + EXTRA] += far_more
            near_part[:rows] += near_more
        else:
            far_part[: rows + EXTRA] = far_more
            near_part[:rows] = near_more
    far_part[rows + 8 : rows + EXTRA] = size[:8] * (0.5 / OFF_WEIGHT)
    near_part[rows:] = far_part[rows:]


def cols_body(images, at, near, far, stats, view, norm, vec, *refs):
    pieces, (near_grad, far_grad, loss, packed, total) = refs[:4], refs[4:]
    blocks, rows, width = near.shape
    half = width // 2
    spot = pl.ds(pl.multiple_of(at[2] * half, half), half)
    size = jnp.zeros((1, half), F32)
    for g in range(blocks):
        for turned in range(4):
            lines = slice(g * (width // 4), (g + 1) * (width // 4))
            packed[g, place(at, turned, width // 4)] = pieces[turned][lines]
        rhs = packed[g]
        square = rhs.astype(F32)
        size = size + jnp.sum(square * square, axis=0, keepdims=True)
        extra = jnp.broadcast_to(stats[g, 4:5], (EXTRA, width)).astype(BF16)
        lhs = jnp.concatenate([near[g], far[g], extra], axis=0)
        part = jnp.dot(lhs, rhs, preferred_element_type=F32)
        if g:
            total[...] += part
        else:
            total[...] = part
    shares = [gather_share(piece[blocks * (width // 4) :, :128]) for piece in pieces]
    loss[...] = (shares[0] + shares[2]) + (shares[1] + shares[3])
    weight = size * (0.5 / OFF_WEIGHT)
    for which, grad in enumerate((near_grad, far_grad)):
        part = slice(which * rows, (which + 1) * rows)
        grad[...] = finish(
            view[part, spot],
            norm[part, spot],
            vec[:, spot],
            total[part],
            total[2 * rows : 2 * rows + 1],
            weight,
            1,
            6,
            images,
        )


def gradient(body, outs, scratch, name, *operands):
    return pl.pallas_call(
        body,
        in_specs=[SMEM] + [VMEM] * (len(operands) - 1),
        out_specs=[VMEM] * len(outs),
        out_shape=outs,
        scratch_shapes=scratch,
        compiler_params=pltpu.CompilerParams(vmem_limit_bytes=10 * MIB),
        cost_estimate=pl.CostEstimate(
            flops=1 << 30, bytes_accessed=7 * MIB, transcendentals=0
        ),
        name=name,
    )(*operands)


def join_body(
    images, at, near, other, loss, other_loss, near_part, far_part, view, norm, vec, grad_a, grad_b, total
):
    rows, half = near.shape
    for which, value in enumerate((near, other)):
        spot = (1 - at[2] if which else at[2]) * half
        grad_b[:, pl.ds(pl.multiple_of(spot, half), half)] = value[...]
    total[...] = loss[...] + other_loss[...]
    ends = near_part[rows:] + far_part[rows:]
    for line in range(0, rows, 64):
        lines = slice(line, line + 64)
        grad_a[lines] = finish(
            view[lines],
            norm[lines],
            vec,
            near_part[lines] + far_part[lines],
            ends[0:1],
            ends[8:9],
            0,
            7,
            images,
        )


def join(images, at, near, *operands):
    rows, half = near.shape
    grad = jax.ShapeDtypeStruct((rows, 2 * half), BF16)
    return pl.pallas_call(
        functools.partial(join_body, images),
        in_specs=[SMEM] + [VMEM] * (1 + len(operands)),
        out_specs=[VMEM] * 3,
        out_shape=[grad, grad, jax.ShapeDtypeStruct((1, 128), F32)],
        compiler_params=pltpu.CompilerParams(vmem_limit_bytes=6 * MIB),
        cost_estimate=pl.CostEstimate(flops=MIB, bytes_accessed=2 * MIB, transcendentals=0),
        name="join",
    )(at, near, *operands)


def local(view_a, view_b):
    rows, width = view_a.shape
    chips = lax.axis_size("y") * lax.axis_size("x")
    blocks = lax.axis_size("z")
    images = rows * 2 * chips
    half = width // 2
    x_at, y_at, c_at, z_at = (lax.axis_index(name) for name in ("x", "y", "c", "z"))
    first_at = jnp.where(c_at == 0, x_at, y_at)
    at = jnp.stack([x_at, y_at, c_at, z_at, first_at]).astype(jnp.int32)

    raw_b = lax.all_gather(view_b, ("c", "z"), axis=0, tiled=False)
    raw_a = lax.all_gather(view_a, "z", axis=0, tiled=False)
    chip_view = jnp.concatenate([view_b, swap(view_b)], axis=0)

    values_a = view_a.astype(F32)
    values_b = view_b.astype(F32)
    local_a = jnp.sum(values_a, axis=0) / rows
    local_b = jnp.sum(values_b, axis=0) / rows
    apart_a = values_a - local_a
    apart_b = values_b - local_b
    mine = jnp.stack(
        [
            local_a,
            local_b,
            jnp.sum(apart_a * apart_a, axis=0),
            jnp.sum(apart_b * apart_b, axis=0),
            jnp.sum(apart_a * apart_b, axis=0),
        ]
    )
    pair = swap(mine)
    gap = mine[:2] - pair[:2]
    joined = jnp.concatenate(
        [
            (mine[:2] + pair[:2]) * 0.5,
            mine[2:4] + pair[2:4] + gap * gap * (rows / 2),
            mine[4:] + pair[4:] + gap[:1] * gap[1:] * (rows / 2),
        ]
    )
    all_stats = spread(joined, PLANE, chips)
    means = jnp.sum(all_stats[:, :2], axis=0) / chips
    away = all_stats[:, :2] - means
    squares = jnp.sum(all_stats[:, 2:4] + 2 * rows * away * away, axis=0)
    cross = jnp.sum(all_stats[:, 4] + 2 * rows * away[:, 0] * away[:, 1], axis=0)
    inverse = lax.rsqrt(squares / images + EPSILON)
    on_diagonal = cross / images * inverse[0] * inverse[1]
    deficit = 1.0 - on_diagonal
    pull_diagonal = lax.reduce_precision(-2.0 * deficit, 8, 7)
    norm_a = rounded(view_a, means[0], inverse[0])
    norm_b = rounded(view_b, means[1], inverse[1])

    left = inverse * (2 * rows * jnp.sum(all_stats[:, :2], axis=0) - images * means)
    stats = jnp.concatenate([means, inverse, left])
    wide_stats = spread(stats, "z", blocks)
    vec = jnp.concatenate([stats[:4], pull_diagonal[None], on_diagonal[None], left])

    chip_a = jnp.concatenate([norm_a, swap(norm_a)], axis=0)
    lhs = rotate(chip_a.T.reshape(4, width // 4, 2 * rows), first_at).reshape(width, 2 * rows)

    diagonal = jnp.sum((deficit * deficit).reshape(4, width // 4), axis=1)
    diagonal = 0.5 * lax.dynamic_slice_in_dim(diagonal, first_at, 1, axis=0)
    diagonal = jnp.broadcast_to(diagonal[None], (1, 128))
    raw_b, wide_stats, lhs, chip_a, chip_view, vec, diagonal = lax.optimization_barrier(
        (raw_b, wide_stats, lhs, chip_a, chip_view, vec, diagonal)
    )
    parts = correlate(at, wide_stats, raw_b, lhs)
    total = parts[0].astype(F32)
    for step in (1, 3, 2):
        total = total + shift(parts[step], step).astype(F32)
    total = total.astype(BF16)
    pull, outward = make_tile(
        at, 2.0 * OFF_WEIGHT / images, diagonal, [total] + others(total, second=True)
    )
    inward = lax.all_to_all(outward, "z", split_axis=0, concat_axis=0, tiled=True)

    ahead, behind, across = others(pull)
    row_pieces = [pull, behind, across, ahead]
    row_pieces, inward, raw_a = lax.optimization_barrier((row_pieces, inward, raw_a))
    inward = compact(inward)
    ahead, behind, across = others(inward)
    col_pieces = [inward, behind, across, ahead]

    wide_a = rounded(raw_a, wide_stats[:, 0:1], wide_stats[:, 2:3])
    far_a = rounded(swap(raw_a), wide_stats[:, 0:1], wide_stats[:, 2:3])

    part = jax.ShapeDtypeStruct((rows + EXTRA, width), F32)
    near_part, far_part = gradient(
        rows_body,
        [part, part],
        [pltpu.VMEM((width, half), BF16)],
        "rows",
        at,
        raw_b,
        wide_stats,
        *row_pieces,
    )
    far_a, far_part = lax.optimization_barrier((far_a, far_part))
    near_grad, far_grad, loss = gradient(
        functools.partial(cols_body, images),
        [jax.ShapeDtypeStruct((rows, half), BF16)] * 2 + [jax.ShapeDtypeStruct((1, 128), F32)],
        [pltpu.VMEM((blocks, width, half), BF16), pltpu.VMEM((2 * rows + EXTRA, half), F32)],
        "cols",
        at,
        wide_a,
        far_a,
        wide_stats,
        chip_view,
        chip_a,
        vec,
        *col_pieces,
    )
    grad_a, grad_b, total_loss = join(
        images,
        at,
        near_grad,
        swap(far_grad),
        loss,
        swap(loss),
        near_part,
        swap(far_part),
        view_a,
        norm_b,
        vec,
    )
    loss_value = total_loss[0, 0]
    return (grad_a, grad_b, loss_value)


def solution(mesh):
    split = P(("y", "x", "c"), "z")
    chips = Mesh(mesh.devices.reshape(4, 4, 2, 8), ("y", "x", "c", "z"))
    return jax.shard_map(
        local,
        mesh=chips,
        in_specs=(split, split),
        out_specs=(split, split, P()),
        check_vma=False,
    )
```

```python
import functools

import jax
import jax.numpy as jnp
from jax import lax
from jax.experimental import pallas as pl
from jax.experimental.pallas import tpu as pltpu
from jax.sharding import Mesh, PartitionSpec as P

OFF_WEIGHT = 0.0051
EPSILON = 1e-05
F32 = jnp.float32
BF16 = jnp.bfloat16
PLANE = ("y", "x")
CONTRACT_LAST = (((1,), (1,)), ((), ()))
EXTRA = 16
MIB = 1 << 20
VMEM = pl.BlockSpec(memory_space=pltpu.VMEM)
SMEM = pl.BlockSpec(memory_space=pltpu.SMEM)


def shift(value, step, second=False):
    y_size, x_size = lax.axis_size("y"), lax.axis_size("x")
    pairs = []
    for y in range(y_size):
        for x in range(x_size):
            for c in range(2):
                along_y = (c == 1) != second
                to_y = (y + step) % y_size if along_y else y
                to_x = x if along_y else (x + step) % x_size
                pairs.append(((y * x_size + x) * 2 + c, (to_y * x_size + to_x) * 2 + c))
    return lax.ppermute(value, ("y", "x", "c"), pairs)


def swap(value):
    return lax.ppermute(value, "c", [(0, 1), (1, 0)])


def spread(value, axes, size):
    copies = jnp.broadcast_to(value[None], (size,) + value.shape)
    return lax.all_to_all(copies, axes, split_axis=0, concat_axis=0, tiled=True)


def rotate(value, by):
    twice = jnp.concatenate([value, value], axis=0)
    return lax.dynamic_slice_in_dim(twice, by, value.shape[0], axis=0)


def others(value, second=False):
    return [shift(value, step, second) for step in (1, 3, 2)]


def normalise(raw, mean, inverse):
    return ((raw.astype(F32) - mean) * inverse).astype(BF16)


def rounded(raw, mean, inverse):
    return lax.reduce_precision((raw.astype(F32) - mean) * inverse, 8, 7).astype(BF16)


def correlate_body(at, stats, raw, lhs, *parts):
    blocks, _, half = parts[0].shape
    quarter = lhs.shape[0] // 4
    cols = pl.ds(pl.multiple_of(at[2] * half, half), half)
    near_at, far_at = at[2] * blocks, (1 - at[2]) * blocks
    for g in range(blocks):
        mean, inverse = stats[g, 1:2, cols], stats[g, 3:4, cols]
        near = normalise(raw[near_at + g, :, cols], mean, inverse)
        far = normalise(raw[far_at + g, :, cols], mean, inverse)
        rhs = jnp.concatenate([near, far], axis=0)
        for turned in range(4):
            part = jnp.dot(
                lhs[turned * quarter : (turned + 1) * quarter],
                rhs,
                preferred_element_type=F32,
            )
            parts[turned][g] = part.astype(BF16)


def correlate(at, stats, raw, lhs):
    both, rows, width = raw.shape
    blocks, half = both // 2, width // 2
    part = jax.ShapeDtypeStruct((blocks, lhs.shape[0] // 4, half), BF16)
    return pl.pallas_call(
        correlate_body,
        in_specs=[SMEM, VMEM, VMEM, VMEM],
        out_specs=[VMEM] * 4,
        out_shape=[part] * 4,
        compiler_params=pltpu.CompilerParams(vmem_limit_bytes=6 * MIB),
        cost_estimate=pl.CostEstimate(
            flops=8 * rows * half * half * blocks, bytes_accessed=6 * MIB, transcendentals=0
        ),
        name="correlate",
    )(at, stats, raw, lhs)


def tile_body(scale, at, diagonal, own, ahead, behind, across, pull, outward):
    blocks, quarter, half = pull.shape
    row = lax.broadcasted_iota(jnp.int32, (quarter, half), 0)
    col = lax.broadcasted_iota(jnp.int32, (quarter, half), 1)
    same = col + at[2] * half == row + at[4] * quarter
    size = jnp.zeros((8, half), F32)
    for g in range(blocks):
        total = (own[g].astype(F32) + across[g].astype(F32)) + (
            ahead[g].astype(F32) + behind[g].astype(F32)
        )
        value = jnp.where(same & (at[3] == g), 0.0, scale * total).astype(BF16)
        pull[g] = value
        outward[g, :quarter] = value
        wide = value.astype(F32)
        size = size + jnp.sum((wide * wide).reshape(quarter // 8, 8, half), axis=0)
    share = diagonal[0:1, 0:1] + (0.25 / OFF_WEIGHT) * jnp.sum(size).reshape(1, 1)
    share = jnp.broadcast_to(share, (EXTRA, half))
    high = share.astype(BF16)
    share = share - high.astype(F32)
    middle = share.astype(BF16)
    low = (share - middle.astype(F32)).astype(BF16)
    line = lax.broadcasted_iota(jnp.int32, (EXTRA, half), 0)
    extra = jnp.where(line == 0, high, jnp.where(line == 1, middle, low))
    for g in range(blocks):
        outward[g, quarter:] = extra


def make_tile(at, scale, diagonal, pieces):
    blocks, quarter, half = pieces[0].shape
    return pl.pallas_call(
        functools.partial(tile_body, scale),
        in_specs=[SMEM] + [VMEM] * 5,
        out_specs=[VMEM] * 2,
        out_shape=[
            jax.ShapeDtypeStruct(pieces[0].shape, BF16),
            jax.ShapeDtypeStruct((blocks, quarter + EXTRA, half), BF16),
        ],
        compiler_params=pltpu.CompilerParams(vmem_limit_bytes=6 * MIB),
        cost_estimate=pl.CostEstimate(
            flops=6 * pieces[0].size, bytes_accessed=3 * MIB, transcendentals=0
        ),
        name="tile",
    )(at, diagonal, *pieces)


def place(at, turned, quarter):
    spot = lax.rem(at[4] + turned, 4) * quarter
    return pl.ds(pl.multiple_of(spot, quarter), quarter)


def finish(view, norm, vec, total, extra, weight, mean_row, left_row, images):
    mean, inverse = vec[mean_row : mean_row + 1], vec[mean_row + 2 : mean_row + 3]
    pull, match, left = vec[4:5], vec[5:6], vec[left_row : left_row + 1]
    back = total + norm.astype(F32) * pull
    centre = (extra + pull * left) * (1.0 / images)
    along = weight + pull * match
    white = (view.astype(F32) - mean) * inverse
    return (inverse * (back - centre - white * along)).astype(BF16)


def gather_share(lines):
    lines = lines.astype(F32)
    return (lines[0:1] + lines[1:2]) + lines[2:3]


def strips(share, half):
    share = jnp.broadcast_to(share, (EXTRA, half))
    high = share.astype(BF16)
    share = share - high.astype(F32)
    middle = share.astype(BF16)
    low = (share - middle.astype(F32)).astype(BF16)
    line = lax.broadcasted_iota(jnp.int32, (EXTRA, half), 0)
    return jnp.where(line == 0, high, jnp.where(line == 1, middle, low))


def compact_body(inward, out):
    blocks, lines, half = inward.shape
    quarter = lines - EXTRA
    share = jnp.zeros((1, half), F32)
    for g in range(blocks):
        out[g * quarter : (g + 1) * quarter] = inward[g, :quarter]
        share = share + gather_share(inward[g, quarter:])
    out[blocks * quarter :] = strips(share, half)


def compact(inward):
    blocks, lines, half = inward.shape
    return pl.pallas_call(
        compact_body,
        in_specs=[VMEM],
        out_specs=VMEM,
        out_shape=jax.ShapeDtypeStruct((blocks * (lines - EXTRA) + EXTRA, half), BF16),
        compiler_params=pltpu.CompilerParams(vmem_limit_bytes=2 * MIB),
        cost_estimate=pl.CostEstimate(flops=1, bytes_accessed=MIB, transcendentals=0),
        name="compact",
    )(inward)


def rows_body(at, raw, stats, *refs):
    pieces, (near_part, far_part, packed) = refs[:4], refs[4:]
    both, rows, width = raw.shape
    blocks, half = both // 2, width // 2
    near_at, far_at = at[2] * blocks, (1 - at[2]) * blocks
    cols = pl.ds(pl.multiple_of(at[2] * half, half), half)
    ones = jnp.ones((EXTRA, half), BF16)
    size = jnp.zeros((EXTRA, width), F32)
    for g in range(blocks):
        for turned in range(4):
            packed[place(at, turned, width // 4)] = pieces[turned][g]
        rhs = packed[...]
        square = rhs.astype(F32)
        square = (square * square).astype(BF16)
        size = size + lax.dot_general(
            ones, square, CONTRACT_LAST, preferred_element_type=F32
        )
        extra = jnp.broadcast_to(stats[g, 5:6, cols], (EXTRA, half)).astype(BF16)
        mean, inverse = stats[g, 1:2, cols], stats[g, 3:4, cols]
        near = normalise(raw[near_at + g, :, cols], mean, inverse)
        far = normalise(raw[far_at + g, :, cols], mean, inverse)
        lhs = jnp.concatenate([far, extra], axis=0)
        far_more = lax.dot_general(lhs, rhs, CONTRACT_LAST, preferred_element_type=F32)
        near_more = lax.dot_general(
            near, rhs, CONTRACT_LAST, preferred_element_type=F32
        )
        if g:
            far_part[: rows + EXTRA] += far_more
            near_part[:rows] += near_more
        else:
            far_part[: rows + EXTRA] = far_more
            near_part[:rows] = near_more
    far_part[rows + 8 : rows + EXTRA] = size[:8] * (0.5 / OFF_WEIGHT)
    near_part[rows:] = far_part[rows:]


def cols_body(images, at, near, far, stats, view, norm, vec, *refs):
    pieces, (near_grad, far_grad, loss, packed, total) = refs[:4], refs[4:]
    blocks, rows, width = near.shape
    half = width // 2
    spot = pl.ds(pl.multiple_of(at[2] * half, half), half)
    size = jnp.zeros((1, half), F32)
    for g in range(blocks):
        for turned in range(4):
            lines = slice(g * (width // 4), (g + 1) * (width // 4))
            packed[g, place(at, turned, width // 4)] = pieces[turned][lines]
        rhs = packed[g]
        square = rhs.astype(F32)
        size = size + jnp.sum(square * square, axis=0, keepdims=True)
        extra = jnp.broadcast_to(stats[g, 4:5], (EXTRA, width)).astype(BF16)
        lhs = jnp.concatenate([near[g], far[g], extra], axis=0)
        part = jnp.dot(lhs, rhs, preferred_element_type=F32)
        if g:
            total[...] += part
        else:
            total[...] = part
    shares = [gather_share(piece[blocks * (width // 4) :, :128]) for piece in pieces]
    sent = strips(((shares[0] + shares[2]) + (shares[1] + shares[3]))[:, :1], half)
    far_grad[rows:] = sent
    loss[...] = gather_share(sent[:, :128])
    weight = size * (0.5 / OFF_WEIGHT)
    for which, grad in enumerate((near_grad, far_grad)):
        part = slice(which * rows, (which + 1) * rows)
        grad[:rows] = finish(
            view[part, spot],
            norm[part, spot],
            vec[:, spot],
            total[part],
            total[2 * rows : 2 * rows + 1],
            weight,
            1,
            6,
            images,
        )


def gradient(body, outs, scratch, name, *operands):
    return pl.pallas_call(
        body,
        in_specs=[SMEM] + [VMEM] * (len(operands) - 1),
        out_specs=[VMEM] * len(outs),
        out_shape=outs,
        scratch_shapes=scratch,
        compiler_params=pltpu.CompilerParams(vmem_limit_bytes=10 * MIB),
        cost_estimate=pl.CostEstimate(
            flops=1 << 30, bytes_accessed=7 * MIB, transcendentals=0
        ),
        name=name,
    )(*operands)


def join_body(
    images, at, near, other, loss, near_part, far_part, view, norm, vec, grad_a, grad_b, total
):
    rows, half = near.shape
    for which, value in enumerate((near, other)):
        spot = (1 - at[2] if which else at[2]) * half
        grad_b[:, pl.ds(pl.multiple_of(spot, half), half)] = value[:rows]
    total[...] = loss[...] + gather_share(other[rows:, :128])
    ends = near_part[rows:] + far_part[rows:]
    for line in range(0, rows, 64):
        lines = slice(line, line + 64)
        grad_a[lines] = finish(
            view[lines],
            norm[lines],
            vec,
            near_part[lines] + far_part[lines],
            ends[0:1],
            ends[8:9],
            0,
            7,
            images,
        )


def join(images, at, near, *operands):
    rows, half = near.shape
    grad = jax.ShapeDtypeStruct((rows, 2 * half), BF16)
    return pl.pallas_call(
        functools.partial(join_body, images),
        in_specs=[SMEM] + [VMEM] * (1 + len(operands)),
        out_specs=[VMEM] * 3,
        out_shape=[grad, grad, jax.ShapeDtypeStruct((1, 128), F32)],
        compiler_params=pltpu.CompilerParams(vmem_limit_bytes=6 * MIB),
        cost_estimate=pl.CostEstimate(flops=MIB, bytes_accessed=2 * MIB, transcendentals=0),
        name="join",
    )(at, near, *operands)


def local(view_a, view_b):
    rows, width = view_a.shape
    chips = lax.axis_size("y") * lax.axis_size("x")
    blocks = lax.axis_size("z")
    images = rows * 2 * chips
    half = width // 2
    x_at, y_at, c_at, z_at = (lax.axis_index(name) for name in ("x", "y", "c", "z"))
    first_at = jnp.where(c_at == 0, x_at, y_at)
    at = jnp.stack([x_at, y_at, c_at, z_at, first_at]).astype(jnp.int32)

    raw_b = lax.all_gather(view_b, ("c", "z"), axis=0, tiled=False)
    raw_a = lax.all_gather(view_a, "z", axis=0, tiled=False)
    chip_view = jnp.concatenate([view_b, swap(view_b)], axis=0)

    values_a = view_a.astype(F32)
    values_b = view_b.astype(F32)
    local_a = jnp.sum(values_a, axis=0) / rows
    local_b = jnp.sum(values_b, axis=0) / rows
    apart_a = values_a - local_a
    apart_b = values_b - local_b
    mine = jnp.stack(
        [
            local_a,
            local_b,
            jnp.sum(apart_a * apart_a, axis=0),
            jnp.sum(apart_b * apart_b, axis=0),
            jnp.sum(apart_a * apart_b, axis=0),
        ]
    )
    pair = swap(mine)
    gap = mine[:2] - pair[:2]
    joined = jnp.concatenate(
        [
            (mine[:2] + pair[:2]) * 0.5,
            mine[2:4] + pair[2:4] + gap * gap * (rows / 2),
            mine[4:] + pair[4:] + gap[:1] * gap[1:] * (rows / 2),
        ]
    )
    all_stats = spread(joined, PLANE, chips)
    means = jnp.sum(all_stats[:, :2], axis=0) / chips
    away = all_stats[:, :2] - means
    squares = jnp.sum(all_stats[:, 2:4] + 2 * rows * away * away, axis=0)
    cross = jnp.sum(all_stats[:, 4] + 2 * rows * away[:, 0] * away[:, 1], axis=0)
    inverse = lax.rsqrt(squares / images + EPSILON)
    on_diagonal = cross / images * inverse[0] * inverse[1]
    deficit = 1.0 - on_diagonal
    pull_diagonal = lax.reduce_precision(-2.0 * deficit, 8, 7)
    norm_a = rounded(view_a, means[0], inverse[0])
    norm_b = rounded(view_b, means[1], inverse[1])

    left = inverse * (2 * rows * jnp.sum(all_stats[:, :2], axis=0) - images * means)
    stats = jnp.concatenate([means, inverse, left])
    wide_stats = spread(stats, "z", blocks)
    vec = jnp.concatenate([stats[:4], pull_diagonal[None], on_diagonal[None], left])

    chip_a = jnp.concatenate([norm_a, swap(norm_a)], axis=0)
    lhs = rotate(chip_a.T.reshape(4, width // 4, 2 * rows), first_at).reshape(width, 2 * rows)

    diagonal = jnp.sum((deficit * deficit).reshape(4, width // 4), axis=1)
    diagonal = 0.5 * lax.dynamic_slice_in_dim(diagonal, first_at, 1, axis=0)
    diagonal = jnp.broadcast_to(diagonal[None], (1, 128))
    raw_b, wide_stats, lhs, chip_a, chip_view, vec, diagonal = lax.optimization_barrier(
        (raw_b, wide_stats, lhs, chip_a, chip_view, vec, diagonal)
    )
    parts = correlate(at, wide_stats, raw_b, lhs)
    total = parts[0].astype(F32)
    for step in (1, 3, 2):
        total = total + shift(parts[step], step).astype(F32)
    total = total.astype(BF16)
    pull, outward = make_tile(
        at, 2.0 * OFF_WEIGHT / images, diagonal, [total] + others(total, second=True)
    )
    inward = lax.all_to_all(outward, "z", split_axis=0, concat_axis=0, tiled=True)

    ahead, behind, across = others(pull)
    row_pieces = [pull, behind, across, ahead]
    row_pieces, inward, raw_a = lax.optimization_barrier((row_pieces, inward, raw_a))
    inward = compact(inward)
    ahead, behind, across = others(inward)
    col_pieces = [inward, behind, across, ahead]

    wide_a = rounded(raw_a, wide_stats[:, 0:1], wide_stats[:, 2:3])
    far_a = rounded(swap(raw_a), wide_stats[:, 0:1], wide_stats[:, 2:3])

    part = jax.ShapeDtypeStruct((rows + EXTRA, width), F32)
    near_part, far_part = gradient(
        rows_body,
        [part, part],
        [pltpu.VMEM((width, half), BF16)],
        "rows",
        at,
        raw_b,
        wide_stats,
        *row_pieces,
    )
    far_a, far_part = lax.optimization_barrier((far_a, far_part))
    near_grad, far_grad, loss = gradient(
        functools.partial(cols_body, images),
        [
            jax.ShapeDtypeStruct((rows, half), BF16),
            jax.ShapeDtypeStruct((rows + EXTRA, half), BF16),
            jax.ShapeDtypeStruct((1, 128), F32),
        ],
        [pltpu.VMEM((blocks, width, half), BF16), pltpu.VMEM((2 * rows + EXTRA, half), F32)],
        "cols",
        at,
        wide_a,
        far_a,
        wide_stats,
        chip_view,
        chip_a,
        vec,
        *col_pieces,
    )
    grad_a, grad_b, total_loss = join(
        images,
        at,
        near_grad,
        swap(far_grad),
        loss,
        near_part,
        swap(far_part),
        view_a,
        norm_b,
        vec,
    )
    loss_value = total_loss[0, 0]
    return (grad_a, grad_b, loss_value)


def solution(mesh):
    split = P(("y", "x", "c"), "z")
    chips = Mesh(mesh.devices.reshape(4, 4, 2, 8), ("y", "x", "c", "z"))
    return jax.shard_map(
        local,
        mesh=chips,
        in_specs=(split, split),
        out_specs=(split, split, P()),
        check_vma=False,
    )
```
